32 devices in a mesh: seq: 4 (over z), dp: 8 (over y, x, core).
Axes of the slice: x: 2, y: 2, z: 4, core: 2. Of those that a mesh axis runs over, the one named last changes fastest.
Arguments:
- tokens: bfloat16 [8, 1024, 1408], P('dp', 'seq'), may hold values from -16 to 16
- weights: bfloat16 [1408, 4, 704], P('dp'), may hold values from -2 to 2
- cotangent: bfloat16 [8, 1024, 1408], P('dp', 'seq'), may hold values from -3 to 3
- col_list: int32 [8, 8, 5], P('dp'), may hold values from 0 to 7, as said below
- cut_lengths: int32 [8, 2], P('dp'), may hold values from 1 to 6, 8 in all within a row
- keep_mask: int32 [8, 1024], P('dp'), may hold values 0 or 1
Outputs:
- sublayer_out: bfloat16 [8, 1024, 1408], P('dp', 'seq')
- grad_tokens: bfloat16 [8, 1024, 1408], P('dp', 'seq')
- grad_weights: float32 [1408, 4, 704], P('dp')
The draws below stay inside these ranges and needn't reach their ends.
Inputs may be any that keep to these rules, and one draw needn't show every extreme that they name: `col_list`: row b lists 5 distinct blocks: b itself first, then blocks within 3 of b, counted cyclically over the packed sequence.
All inputs are finite; a program needn't handle non-finite values. No bound on the sum of `keep_mask` on one device may be relied on, other than what follows from the above.
Results may differ from the reference program's by a relative error of at most 0.038.
Values may be sent and summed in bfloat16 or wider, within the bound.
No kernel may reach another device: no remote copies, remote signals or barrier semaphores. Data moves between devices by JAX's collectives and lax.ppermute only.
A program may use at most 128 MiB of HBM per device.

```python
import math
import jax
import jax.numpy as jnp
import numpy as np
from jax import lax

D = 1408
HD = 88
HEADS = 8
HH = 704
NNZ = 5
WIN = 3
SEQLEN = 1024
NBLK = 8
NCUT = 2
MAXCUT = 6
N_DP = 8


def draw_tokens(key, part):
    shape = (N_DP, SEQLEN, D)
    return jnp.clip(jax.random.normal(key, shape, jnp.float32), -6.0, 6.0).astype(jnp.bfloat16)


def draw_weights(key, part):
    key_a, key_b = jax.random.split(key, 2)
    inner = jnp.clip(jax.random.normal(key_a, (D, 3, HH), jnp.float32), -6.0, 6.0) * D ** (-0.5)
    outer = jnp.clip(jax.random.normal(key_b, (D, 1, HH), jnp.float32), -6.0, 6.0) * HH ** (-0.5)
    return jnp.concatenate([inner, outer], axis=1).astype(jnp.bfloat16)


def draw_col_list(key, part):
    rows = N_DP * NBLK
    keys_many = jax.random.split(key, rows)
    orders = jax.vmap(lambda single: jax.random.permutation(single, 2 * WIN))(keys_many).astype(jnp.int32)
    offsets = jnp.where(orders < WIN, orders - WIN, orders - WIN + 1)[:, :NNZ - 1]
    offsets = offsets.reshape(N_DP, NBLK, NNZ - 1)
    blocks = jnp.broadcast_to(jnp.arange(NBLK, dtype=jnp.int32)[None, :, None], (N_DP, NBLK, 1))
    others = (blocks + offsets + NBLK) % NBLK
    return jnp.concatenate([blocks, others], axis=2).astype(jnp.int32)


def place_ends(values, own_key, smallest, high):
    index_at = [jax.random.randint(jax.random.fold_in(own_key, axis), (), 0, length) for axis, length in enumerate(values.shape)]
    longest = values.shape.index(max(values.shape))
    beside = index_at[:longest] + [(index_at[longest] + 1) % values.shape[longest]] + index_at[longest + 1:]
    return values.at[tuple(index_at)].set(smallest).at[tuple(beside)].set(high)


def strengthened(entries, key, source, target, shards_of, factor):
    owner, partner = [(jnp.arange(entries.shape[axis_at]) // (entries.shape[axis_at] // shards_of)).reshape([-1 if axis == axis_at else 1 for axis in range(entries.ndim)]) for axis_at in (source, target)]
    chosen = jax.random.permutation(key, shards_of)[partner]
    strong = (owner == chosen) | (owner == (partner + shards_of // 2) % shards_of)
    return jnp.where(strong, factor * entries, entries)


def levels(own_key, shape, shards, smallest, high):
    factor_of, own = 1.0, jax.random.fold_in(own_key, 6)
    for position, shards_of in shards:
        steps = jnp.exp(jax.random.uniform(jax.random.fold_in(own, position), (shards_of,), jnp.float32, smallest / len(shards), high / len(shards)))
        factor_of = factor_of * jnp.repeat(steps, shape[position] // shards_of).reshape([-1 if axis == position else 1 for axis in range(len(shape))])
    return factor_of


def split_up(number_of, total, limit, slope):
    portions = [(1 << 20) // math.isqrt(standing ** slope) + 1 for standing in range(2, number_of + 1)]
    rest, counts = total - limit - (number_of - 1), [1] * (number_of - 1)
    while rest > 0:
        movable = [i for i in range(number_of - 1) if counts[i] < limit]
        pool, budget = sum([portions[i] for i in movable]), rest
        for i in movable:
            extra = min(limit - counts[i], max(1, budget * portions[i] // pool), rest)
            counts[i] = counts[i] + extra
            rest = rest - extra
    return np.array([limit] + counts)


def uneven(stream_key, number_of, total, bound, slope):
    if number_of == 2:
        one = jax.random.randint(stream_key, (), max(1, total - bound), min(bound, total - 1) + 1)
        return jnp.stack([one, total - one])
    sizes = jnp.asarray(split_up(number_of, total, bound, slope), jnp.int32)
    twos = (number_of - 1) // 2
    donor, sink = sizes[1:1 + 2 * twos:2], sizes[2:2 + 2 * twos:2]
    room = jnp.minimum(donor - 1, bound - sink)
    shifted = jax.random.randint(jax.random.fold_in(stream_key, 1), (twos,), 0, 1 << 20) % (room + 1)
    sizes = sizes.at[1:1 + 2 * twos:2].set(donor - shifted).at[2:2 + 2 * twos:2].set(sink + shifted)
    return sizes[jax.random.permutation(jax.random.fold_in(stream_key, 2), number_of)]


def bell_draw_with(key, shape, deviation, reach, shards, heavy, held_as=jnp.bfloat16):
    array = deviation * jax.random.normal(key, shape, jnp.float32)
    if shards:
        array = array * levels(key, shape, shards, -0.22, 0.18)
    return jnp.clip(strengthened(array, jax.random.fold_in(key, 3), *heavy), -reach, reach).astype(held_as)


def setup_inputs(seed: int = 0) -> dict:
    splits = jax.random.split(jax.random.key(seed), 7)
    tokens = draw_tokens(jax.random.fold_in(splits[6], 71), 0)
    weights = draw_weights(jax.random.fold_in(splits[6], 71), 0)
    cotangent = bell_draw_with(splits[2], (N_DP, SEQLEN, D), 0.5, 3.0, ((0, 8), (1, 4)), (0, 2, 8, 2.0))
    col_list = draw_col_list(jax.random.fold_in(splits[6], 71), 0)
    cut_lengths = jax.vmap(lambda own: uneven(own, NCUT, NBLK, MAXCUT, 2))(jax.random.split(splits[4], N_DP)).reshape((N_DP, NCUT)).astype(jnp.int32)
    keep_mask = place_ends((jax.random.randint(splits[5], (N_DP, SEQLEN), 0, 4) < 3).astype(jnp.int32), jax.random.fold_in(splits[5], 1), 0, 1)
    return dict(tokens=tokens, weights=weights, cotangent=cotangent, col_list=col_list, cut_lengths=cut_lengths, keep_mask=keep_mask)


def block_owner(lengths, count):
    ends = jnp.cumsum(lengths, dtype=jnp.int32)
    index = jnp.arange(count, dtype=jnp.int32)
    return lax.optimization_barrier(jnp.sum((ends[None, :] <= index[:, None]).astype(jnp.int32), axis=1, dtype=jnp.int32))

def allowed_pairs(columns, owner, keep_blocks):
    count, listed = columns.shape
    width = keep_blocks.shape[1]
    same = owner[columns] == owner[:, None]
    kept = keep_blocks[columns] == 1
    itself = columns == jnp.arange(count, dtype=jnp.int32)[:, None]
    diagonal = jnp.eye(width, dtype=bool)
    return same[:, None, :, None] & (kept[:, None, :, :] | itself[:, None, :, None] & diagonal[None, :, None, :])

def attend(query_rows, key_rows, value_rows, columns, allowed, heads):
    length = query_rows.shape[0]
    count = columns.shape[0]
    width = length // count
    scale = 1.0 / math.sqrt(HD)
    query_blk = query_rows.reshape(count, width, heads, HD)
    key_blk = key_rows.reshape(count, width, heads, HD)[columns]
    value_blk = value_rows.reshape(count, width, heads, HD)[columns]
    scores = jnp.einsum('bqhd,bnkhd->bhqnk', query_blk.astype(jnp.float32), key_blk.astype(jnp.float32)) * scale
    scores = jnp.where(allowed[:, None], scores, -jnp.inf)
    largest = lax.optimization_barrier(jnp.max(scores, axis=(3, 4), keepdims=True))
    expd = jnp.exp(scores - largest)
    probs = expd / lax.optimization_barrier(jnp.sum(expd, axis=(3, 4), keepdims=True))
    probs_low = probs.astype(jnp.bfloat16)
    attended = jnp.einsum('bhqnk,bnkhd->bqhd', probs_low.astype(jnp.float32), value_blk.astype(jnp.float32))
    attended = attended.astype(jnp.bfloat16).reshape(length, heads * HD)
    return (attended, probs, probs_low, query_blk, key_blk, value_blk)

def attend_back(d_attended, attended, probs, probs_low, query_blk, key_blk, value_blk, columns):
    count, width, heads, size = query_blk.shape
    scale = 1.0 / math.sqrt(HD)
    d_blk = d_attended.reshape(count, width, heads, size)
    out_blk = attended.reshape(count, width, heads, size)
    delta = lax.optimization_barrier(jnp.sum(d_blk.astype(jnp.float32) * out_blk.astype(jnp.float32), axis=3))
    delta = jnp.transpose(delta, (0, 2, 1))[:, :, :, None, None]
    d_probs = jnp.einsum('bqhd,bnkhd->bhqnk', d_blk.astype(jnp.float32), value_blk.astype(jnp.float32))
    d_scores = (probs * (d_probs - delta) * scale).astype(jnp.bfloat16)
    d_query = jnp.einsum('bhqnk,bnkhd->bqhd', d_scores.astype(jnp.float32), key_blk.astype(jnp.float32))
    d_query = d_query.astype(jnp.bfloat16).reshape(count * width, heads * size)
    d_key_blk = jnp.einsum('bhqnk,bqhd->bnkhd', d_scores.astype(jnp.float32), query_blk.astype(jnp.float32))
    d_value_blk = jnp.einsum('bhqnk,bqhd->bnkhd', probs_low.astype(jnp.float32), d_blk.astype(jnp.float32))
    empty = jnp.zeros((count, width, heads, size), jnp.float32)
    d_key = empty.at[columns].add(d_key_blk).astype(jnp.bfloat16).reshape(count * width, heads * size)
    d_value = empty.at[columns].add(d_value_blk).astype(jnp.bfloat16).reshape(count * width, heads * size)
    return (d_query, d_key, d_value)

def replica(tokens_r, cotangent_r, columns, lengths, keep_r, weights):
    count = columns.shape[0]
    owner = block_owner(lengths, count)
    allowed = allowed_pairs(columns, owner, keep_r.reshape(count, -1))
    inner = weights[:, :3, :].astype(jnp.float32)
    outer = weights[:, 3, :]
    projected = jnp.einsum('td,dch->cth', tokens_r.astype(jnp.float32), inner).astype(jnp.bfloat16)
    attended, probs, probs_low, query_blk, key_blk, value_blk = attend(projected[0], projected[1], projected[2], columns, allowed, HEADS)
    result = jnp.dot(attended, outer.T, preferred_element_type=jnp.float32).astype(jnp.bfloat16)
    d_attended = jnp.dot(cotangent_r, outer, preferred_element_type=jnp.float32).astype(jnp.bfloat16)
    d_query, d_key, d_value = attend_back(d_attended, attended, probs, probs_low, query_blk, key_blk, value_blk, columns)
    d_proj = jnp.stack([d_query, d_key, d_value], axis=0)
    grad_in = jnp.einsum('cth,dch->td', d_proj.astype(jnp.float32), inner).astype(jnp.bfloat16)
    grad_inner = jnp.einsum('td,cth->dch', tokens_r.astype(jnp.float32), d_proj.astype(jnp.float32))
    grad_outer = jnp.dot(cotangent_r.T, attended, preferred_element_type=jnp.float32)
    grad_all = jnp.concatenate([grad_inner, grad_outer[:, None, :]], axis=1)
    return (result, grad_in, grad_all)

def reference(tokens, weights, cotangent, col_list, cut_lengths, keep_mask):

    def step(total, items):
        tokens_r, cotangent_r, columns, lengths, keep_r = items
        result, grad_in, grad_all = replica(tokens_r, cotangent_r, columns, lengths, keep_r, weights)
        return (total + grad_all, (result, grad_in))
    start = jnp.zeros((weights.shape[0], 4, weights.shape[2]), jnp.float32)
    total, stacked = lax.scan(step, start, (tokens, cotangent, col_list, cut_lengths, keep_mask))
    return (stacked[0], stacked[1], total / N_DP)
```

```python
import functools
import math

import jax
import jax.numpy as jnp
from jax import lax
from jax.experimental import pallas as pl
from jax.experimental.pallas import tpu as pltpu
from jax.sharding import PartitionSpec as P

HD = 88
SCALE = 1.0 / math.sqrt(HD)
LOW = -1e30
F32 = jnp.float32
BF16 = jnp.bfloat16


def shifted(array, step):
    count = lax.axis_size("seq")
    return lax.ppermute(array, "seq", [(i, (i + step) % count) for i in range(count)])


def exchanged(array, bit):
    count = lax.axis_size("dp")
    return lax.ppermute(array, "dp", [(i, i ^ bit) for i in range(count)])


def bit_orders(count):
    far = [1 << i for i in range(1, count.bit_length() - 1)]
    half = len(far) // 2
    return far, far[half:] + far[:half]


def gather_rows(block, bits):
    index = lax.axis_index("dp")
    held, total = [], block
    for bit in bits:
        other = exchanged(total, bit)
        upper = (index & bit) != 0
        low = jnp.where(upper, other, total)
        high = jnp.where(upper, total, other)
        total = jnp.stack([low, high], axis=sum(1 for seen in held if seen > bit))
        held.append(bit)
    return total.reshape(-1, block.shape[-1])


def scatter_rows(total, bits):
    index = lax.axis_index("dp")
    held = sorted(bits, reverse=True)
    rows = total.shape[0] >> len(bits)
    total = total.reshape((2,) * len(bits) + (rows, total.shape[1]))
    for bit in bits:
        axis = held.index(bit)
        low = lax.index_in_dim(total, 0, axis, keepdims=False)
        high = lax.index_in_dim(total, 1, axis, keepdims=False)
        upper = (index & bit) != 0
        sent = jnp.where(upper, low, high).astype(BF16)
        kept = jnp.where(upper, high, low).astype(F32)
        total = kept + exchanged(sent, bit).astype(F32)
        held.remove(bit)
    return total


def chain(block):
    count = lax.axis_size("seq")
    z = lax.axis_index("seq")
    ups, downs = [block], [block]
    for hop in range(1, count):
        downs.append(
            lax.ppermute(downs[-1], "seq", [(i, i + 1) for i in range(hop - 1, count - 1)])
        )
        ups.append(
            lax.ppermute(ups[-1], "seq", [(i, i - 1) for i in range(1, count - hop + 1)])
        )
    return [block] + [
        jnp.where(z + k < count, ups[k], downs[count - k]) for k in range(1, count)
    ]


def forward_kernel(parts, heads, count, cols, same, bias, *refs):
    qkv, (att_out, probs_out) = refs[:parts], refs[parts : parts + 2]
    keys, vals = refs[parts + 2 :]
    width = qkv[0].shape[2]
    for k in range(parts):
        span = slice(k * width, (k + 1) * width)
        for h in range(heads):
            keys[h, :, span] = qkv[k][heads + h]
            vals[h, span, :] = qkv[k][2 * heads + h].astype(F32).T.astype(BF16)
    per = count // parts
    listed = cols.shape[1]
    rows = lax.broadcasted_iota(jnp.int32, (128, 128), 0)
    lanes = lax.broadcasted_iota(jnp.int32, (128, 128), 1)
    diagonal = rows == lanes
    for part in range(parts):

        @pl.loop(0, per)
        def _(step):
            b = part * per + step
            at = pl.ds(pl.multiple_of(step * 128, 128), 128)
            spots = [cols[b, n] for n in range(listed)]
            pens = [
                bias[spots[n]] + jnp.where(same[b, n] == 1, 0.0, LOW) for n in range(listed)
            ]
            first = jnp.where(diagonal, 0.0, jnp.broadcast_to(pens[0], (128, 128)))
            for h in range(heads):
                query = qkv[part][h, :, at].astype(F32).T.astype(BF16)
                key_t = jnp.concatenate(
                    [keys[h, :, pl.ds(pl.multiple_of(s * 128, 128), 128)] for s in spots], axis=1
                )
                val = jnp.concatenate(
                    [vals[h, pl.ds(pl.multiple_of(s * 128, 128), 128), :] for s in spots], axis=0
                )
                scores = jnp.dot(query, key_t, preferred_element_type=F32) * SCALE
                scores = jnp.concatenate(
                    [scores[:, :128] + first]
                    + [scores[:, n * 128 : (n + 1) * 128] + pens[n] for n in range(1, listed)],
                    axis=1,
                )
                largest = jnp.max(scores, axis=1, keepdims=True)
                expd = jnp.exp(scores - largest)
                probs = expd * (1.0 / jnp.sum(expd, axis=1, keepdims=True))
                probs = probs.astype(BF16)
                probs_out[h, b] = probs
                att = jnp.dot(probs, val, preferred_element_type=F32)
                att_out[part, h, :, at] = att.T.astype(BF16)


def backward_kernel(parts, heads, count, cols, *refs):
    qkv, d_att = refs[:parts], refs[parts : 2 * parts]
    probs_in = refs[2 * parts]
    out = refs[2 * parts + 1]
    keys, keys_t, vals_t, acc_k, acc_v = refs[2 * parts + 2 :]
    width = qkv[0].shape[2]
    for k in range(parts):
        span = slice(k * width, (k + 1) * width)
        for h in range(heads):
            keys[h, span, :] = qkv[k][heads + h].astype(F32).T.astype(BF16)
            keys_t[h, :, span] = qkv[k][heads + h]
            vals_t[h, :, span] = qkv[k][2 * heads + h]
    acc_k[...] = jnp.zeros_like(acc_k)
    acc_v[...] = jnp.zeros_like(acc_v)
    per = count // parts
    listed = cols.shape[1]
    for part in range(parts):

        @pl.loop(0, per)
        def _(step):
            b = part * per + step
            at = pl.ds(pl.multiple_of(step * 128, 128), 128)
            spots = [
                pl.ds(pl.multiple_of(cols[b, n] * 128, 128), 128) for n in range(listed)
            ]
            for h in range(heads):
                d_t = d_att[part][h, :, at]
                query_t = qkv[part][h, :, at]
                val_t = jnp.concatenate([vals_t[h, :, s] for s in spots], axis=1)
                key = jnp.concatenate([keys[h, s, :] for s in spots], axis=0)
                d_probs = jnp.dot(
                    d_t.astype(F32).T.astype(BF16), val_t, preferred_element_type=F32
                )
                probs_low = probs_in[h, b]
                probs = probs_low.astype(F32)
                weighted = probs * d_probs
                delta = jnp.sum(weighted, axis=1, keepdims=True)
                d_scores = ((weighted - probs * delta) * SCALE).astype(BF16)
                d_query = jnp.dot(d_scores, key, preferred_element_type=F32)
                out[part, h, :, at] = d_query.T.astype(BF16)
                d_key = jnp.dot(query_t, d_scores, preferred_element_type=F32)
                d_val = jnp.dot(d_t, probs_low, preferred_element_type=F32)
                for n in range(listed):
                    acc_k[h, :, spots[n]] += d_key[:, n * 128 : (n + 1) * 128]
                    acc_v[h, :, spots[n]] += d_val[:, n * 128 : (n + 1) * 128]

    for k in range(parts):
        span = slice(k * width, (k + 1) * width)
        for h in range(heads):
            out[k, heads + h] = acc_k[h, :, span].astype(BF16)
            out[k, 2 * heads + h] = acc_v[h, :, span].astype(BF16)


def attend(qkv, cols, same, bias):
    parts, heads = len(qkv), qkv[0].shape[0] // 3
    width = qkv[0].shape[2]
    count, listed = cols.shape
    length = width * parts
    smem = pl.BlockSpec(memory_space=pltpu.SMEM)
    vmem = pl.BlockSpec(memory_space=pltpu.VMEM)
    return pl.pallas_call(
        functools.partial(forward_kernel, parts, heads, count),
        out_shape=(
            jax.ShapeDtypeStruct((parts, heads, HD, width), BF16),
            jax.ShapeDtypeStruct((heads, count, 128, listed * 128), BF16),
        ),
        in_specs=[smem, smem, vmem] + [vmem] * parts,
        out_specs=(vmem, vmem),
        scratch_shapes=[
            pltpu.VMEM((heads, HD, length), BF16),
            pltpu.VMEM((heads, length, HD), BF16),
        ],
        compiler_params=pltpu.CompilerParams(vmem_limit_bytes=40 << 20),
        name="attend",
    )(cols, same, bias, *qkv)


def attend_back(qkv, d_att, probs, cols):
    parts, heads = len(qkv), qkv[0].shape[0] // 3
    width = qkv[0].shape[2]
    count = cols.shape[0]
    length = width * parts
    smem = pl.BlockSpec(memory_space=pltpu.SMEM)
    vmem = pl.BlockSpec(memory_space=pltpu.VMEM)
    return pl.pallas_call(
        functools.partial(backward_kernel, parts, heads, count),
        out_shape=jax.ShapeDtypeStruct((parts, 3 * heads, HD, width), BF16),
        in_specs=[smem] + [vmem] * (2 * parts + 1),
        out_specs=vmem,
        scratch_shapes=[
            pltpu.VMEM((heads, length, HD), BF16),
            pltpu.VMEM((heads, HD, length), BF16),
            pltpu.VMEM((heads, HD, length), BF16),
            pltpu.VMEM((heads, HD, length), F32),
            pltpu.VMEM((heads, HD, length), F32),
        ],
        compiler_params=pltpu.CompilerParams(vmem_limit_bytes=40 << 20),
        name="attend_back",
    )(cols, *qkv, *d_att, probs)


def dot(left, right, axes):
    return lax.dot_general(left, right, (axes, ((), ())), preferred_element_type=F32)


def body(tokens, weights, cotangent, col_list, cut_lengths, keep_mask):
    parts, replicas = lax.axis_size("seq"), lax.axis_size("dp")
    z = lax.axis_index("seq")
    inputs, upstream = tokens[0], cotangent[0]
    rows = weights.shape[0]
    group = weights.shape[2] // parts
    heads = group // HD
    order_a, order_b = bit_orders(replicas)

    pieces = chain(inputs)

    split = weights.reshape(rows, 4, parts, group)
    split = jnp.concatenate([split, split], axis=2)
    split = lax.dynamic_slice_in_dim(split, z, parts, axis=2)
    outer_shard = split[:, 3].reshape(rows, parts * group)
    inner_shard = split[:, :3]
    half = parts // 2 * group
    outer = jnp.concatenate(
        [
            gather_rows(outer_shard[:, :half], order_a + [1]),
            gather_rows(outer_shard[:, half:], order_b + [1]),
        ],
        axis=1,
    )
    inner = [
        gather_rows(
            inner_shard[:, :, j].reshape(rows, 3 * group), (order_b if j % 2 else order_a) + [1]
        )
        for j in range(parts)
    ]

    columns = col_list[0]
    count = columns.shape[0]
    turn = z * (count // parts)
    columns = jnp.roll((columns - turn) % count, -turn, axis=0)
    ends = jnp.cumsum(cut_lengths[0])
    index = (jnp.arange(count, dtype=jnp.int32) + turn) % count
    owner = jnp.sum((ends[None, :] <= index[:, None]).astype(jnp.int32), axis=1)
    same = (owner[columns] == owner[:, None]).astype(jnp.int32)
    bias = jnp.where(jnp.roll(keep_mask[0].reshape(count, 1, -1), -turn, axis=0) == 1, 0.0, LOW)

    d_all = dot(outer, upstream, ((0,), (1,))).astype(BF16)
    d_own = [d_all[k * group : (k + 1) * group] for k in range(parts)]
    d_att = [d_own[0]] + [shifted(d_own[parts - k], parts - k) for k in range(1, parts)]
    d_att = [d.reshape(heads, HD, -1) for d in d_att]

    qkv = [
        dot(inner[0], piece, ((0,), (1,))).astype(BF16).reshape(3 * heads, HD, -1)
        for piece in pieces
    ]
    att, probs = attend(qkv, columns, same, bias)
    att = att.reshape(parts, group, -1)
    att_here = [att[0]] + [shifted(att[parts - j], parts - j) for j in range(1, parts)]
    att_here = jnp.concatenate(att_here, axis=0)
    result = dot(att_here, outer, ((0,), (1,))).astype(BF16)
    outer_part = dot(upstream, att_here, ((0,), (1,)))

    d_qkv = attend_back(qkv, d_att, probs, columns)
    d_qkv = d_qkv.reshape(parts, 3 * group, -1)
    d_here = [d_qkv[0]] + [shifted(d_qkv[parts - j], parts - j) for j in range(1, parts)]
    grad_in = sum(dot(d_here[j], inner[j], ((0,), (1,))) for j in range(parts)).astype(BF16)

    all_rows = jnp.concatenate(pieces, axis=0)
    d_rows = jnp.concatenate([d_qkv[k] for k in range(parts)], axis=1)
    inner_part = dot(all_rows, d_rows, ((0,), (1,)))

    cut = 3 * group // 2
    inner_sum = jnp.concatenate(
        [
            scatter_rows(inner_part[:, :cut], [1] + order_a),
            scatter_rows(inner_part[:, cut:], [1] + order_b),
        ],
        axis=1,
    )
    outer_sum = jnp.concatenate(
        [
            scatter_rows(outer_part[:, :half], [1] + order_a),
            scatter_rows(outer_part[:, half:], [1] + order_b),
        ],
        axis=1,
    )
    outer_low = outer_sum.astype(BF16)
    outer_own = outer_sum[:, :group]
    for j in range(1, parts):
        outer_own = outer_own + shifted(
            outer_low[:, j * group : (j + 1) * group], j
        ).astype(F32)
    own = jnp.concatenate([inner_sum, outer_own], axis=1).astype(BF16)
    found = [own] + [shifted(own, parts - j) for j in range(1, parts)]
    found = jnp.stack(found + found, axis=0)
    found = lax.dynamic_slice_in_dim(found, (parts - z) % parts, parts, axis=0)
    found = found.reshape(parts, rows, 4, group)
    grad_all = jnp.transpose(found, (1, 2, 0, 3)).reshape(rows, 4, parts * group)
    grad_all = grad_all.astype(F32) / replicas
    return (result[None], grad_in[None], grad_all)


def solution(mesh):
    placed = (
        P("dp", "seq", None),
        P("dp", None, None),
        P("dp", "seq", None),
        P("dp", None, None),
        P("dp", None),
        P("dp", None),
    )
    return jax.shard_map(
        body,
        mesh=mesh,
        in_specs=placed,
        out_specs=(P("dp", "seq", None), P("dp", "seq", None), P("dp", None, None)),
        check_vma=False,
    )
```

```python
import functools
import math

import jax
import jax.numpy as jnp
from jax import lax
from jax.experimental import pallas as pl
from jax.experimental.pallas import tpu as pltpu
from jax.sharding import PartitionSpec as P

HD = 88
SCALE = 1.0 / math.sqrt(HD)
LOW = -1e30
F32 = jnp.float32
BF16 = jnp.bfloat16


def shifted(array, step):
    count = lax.axis_size("seq")
    return lax.ppermute(array, "seq", [(i, (i + step) % count) for i in range(count)])


def exchanged(array, bit):
    count = lax.axis_size("dp")
    return lax.ppermute(array, "dp", [(i, i ^ bit) for i in range(count)])


def bit_orders(count):
    far = [1 << i for i in range(1, count.bit_length() - 1)]
    half = len(far) // 2
    return far, far[half:] + far[:half]


def gather_shards(block, bits):
    held = {0: block}
    for bit in bits:
        held.update({r | bit: exchanged(part, bit) for r, part in list(held.items())})
    return [held[r] for r in sorted(held)]


def in_order_kernel(index, *refs):
    pieces, out = refs[:-1], refs[-1]
    for r, piece in enumerate(pieces):
        out[index[0] ^ r] = piece[...]


def in_order(pieces, index):
    rows, columns = pieces[0].shape
    vmem = pl.BlockSpec(memory_space=pltpu.VMEM)
    return pl.pallas_call(
        in_order_kernel,
        out_shape=jax.ShapeDtypeStruct((len(pieces), rows, columns), BF16),
        in_specs=[pl.BlockSpec(memory_space=pltpu.SMEM)] + [vmem] * len(pieces),
        out_specs=vmem,
        compiler_params=pltpu.CompilerParams(vmem_limit_bytes=40 << 20),
        name="in_order",
    )(index, *pieces).reshape(len(pieces) * rows, columns)


def shard_kernel(parts, place, weights, low, high):
    group = weights.shape[2] // parts
    half = low.shape[1]
    for z in range(parts):

        @pl.when(place[0] == z)
        def _():
            cols = [weights[:, c, :] for c in range(4)]

            def block(c, j):
                start = (z + j) % parts * group
                return cols[c][:, start : start + group]

            chosen = [block(c, 0) for c in range(3)] + [block(3, j) for j in range(parts)]
            chosen += [block(c, j) for j in range(1, parts) for c in range(3)]
            middle = half // group
            low[...] = jnp.concatenate(chosen[:middle], axis=1)
            high[...] = jnp.concatenate(chosen[middle:], axis=1)


def ordered_shard(weights, place, parts):
    rows, _, columns = weights.shape
    vmem = pl.BlockSpec(memory_space=pltpu.VMEM)
    shape = jax.ShapeDtypeStruct((rows, 2 * columns), BF16)
    return pl.pallas_call(
        functools.partial(shard_kernel, parts),
        out_shape=(shape, shape),
        in_specs=[pl.BlockSpec(memory_space=pltpu.SMEM), vmem],
        out_specs=(vmem, vmem),
        compiler_params=pltpu.CompilerParams(vmem_limit_bytes=40 << 20),
        name="ordered_shard",
    )(place, weights)


def gradient_kernel(count, index, *refs):
    lefts, rights = refs[:count], refs[count : 2 * count]
    sent, kept, whole = refs[2 * count :]
    shards, rows, _ = sent.shape
    step = 128
    width = rights[0].shape[1]
    for start in range(0, width, step):
        total = None
        for left, right in zip(lefts, rights):
            part = jnp.dot(left[...], right[:, start : start + step], preferred_element_type=F32)
            total = part if total is None else total + part
        whole[start : start + step, :] = total.T
    for r in range(shards):
        mine = index[0] ^ (2 * r)
        kept[r] = whole[pl.ds(pl.multiple_of(mine * rows, 8), rows), :]
        other = mine ^ 1
        sent[r] = whole[pl.ds(pl.multiple_of(other * rows, 8), rows), :].astype(BF16)


def gradient_halves(lefts, rights, index, replicas):
    columns, width = lefts[0].shape[0], rights[0].shape[1]
    rows = width // replicas
    vmem = pl.BlockSpec(memory_space=pltpu.VMEM)
    shape = (replicas // 2, rows, columns)
    return pl.pallas_call(
        functools.partial(gradient_kernel, len(lefts)),
        out_shape=(jax.ShapeDtypeStruct(shape, BF16), jax.ShapeDtypeStruct(shape, F32)),
        in_specs=[pl.BlockSpec(memory_space=pltpu.SMEM)] + [vmem] * (2 * len(lefts)),
        out_specs=(vmem, vmem),
        scratch_shapes=[pltpu.VMEM((width, columns), F32)],
        compiler_params=pltpu.CompilerParams(vmem_limit_bytes=40 << 20),
        name="gradient_halves",
    )(index, *lefts, *rights)


def scatter_far(blocks, bits):
    held = {2 * r: blocks[r] for r in range(blocks.shape[0])}
    for bit in bits:
        given = [r for r in held if r & bit]
        kept = [r for r in held if not r & bit]
        arrived = exchanged(jnp.stack([held[r] for r in given]).astype(BF16), bit).astype(F32)
        held = {r: held[r] + arrived[given.index(r | bit)] for r in kept}
    return held[0]


def scatter_rows(sent, kept, orders):
    total = kept + exchanged(sent, 1).astype(F32)
    cut = (kept.shape[1] // 2 + 15) // 16 * 16
    return jnp.concatenate(
        [scatter_far(total[:, :cut], orders[0]), scatter_far(total[:, cut:], orders[1])], axis=0
    )


def final_kernel(parts, replicas, place, *refs):
    found, out = refs[:-1], refs[-1]
    group = out.shape[2] // parts
    for z in range(parts):

        @pl.when(place[0] == z)
        def _():
            for c in range(4):
                span = slice(c * group, (c + 1) * group)
                out[:, c, :] = jnp.concatenate(
                    [found[(hg - z) % parts][:, span].astype(F32) for hg in range(parts)], axis=1
                ) * (1.0 / replicas)


def final_rows(found, place, replicas):
    parts = len(found)
    rows, columns = found[0].shape
    vmem = pl.BlockSpec(memory_space=pltpu.VMEM)
    return pl.pallas_call(
        functools.partial(final_kernel, parts, replicas),
        out_shape=jax.ShapeDtypeStruct((rows, 4, columns // 4 * parts), F32),
        in_specs=[pl.BlockSpec(memory_space=pltpu.SMEM)] + [vmem] * parts,
        out_specs=vmem,
        compiler_params=pltpu.CompilerParams(vmem_limit_bytes=40 << 20),
        name="final_rows",
    )(place, *found)


def chain(block):
    count = lax.axis_size("seq")
    z = lax.axis_index("seq")
    ups, downs = [block], [block]
    for hop in range(1, count):
        downs.append(
            lax.ppermute(downs[-1], "seq", [(i, i + 1) for i in range(hop - 1, count - 1)])
        )
        ups.append(
            lax.ppermute(ups[-1], "seq", [(i, i - 1) for i in range(1, count - hop + 1)])
        )
    return [block] + [
        jnp.where(z + k < count, ups[k], downs[count - k]) for k in range(1, count)
    ]


def forward_kernel(parts, heads, count, cols, same, bias, *refs):
    qkv, (att_out, probs_out) = refs[:parts], refs[parts : parts + 2]
    keys, vals = refs[parts + 2 :]
    width = qkv[0].shape[2]
    for k in range(parts):
        span = slice(k * width, (k + 1) * width)
        for h in range(heads):
            keys[h, :, span] = qkv[k][heads + h]
            vals[h, span, :] = qkv[k][2 * heads + h].astype(F32).T.astype(BF16)
    per = count // parts
    listed = cols.shape[1]
    rows = lax.broadcasted_iota(jnp.int32, (128, 128), 0)
    lanes = lax.broadcasted_iota(jnp.int32, (128, 128), 1)
    diagonal = rows == lanes
    for part in range(parts):

        @pl.loop(0, per)
        def _(step):
            b = part * per + step
            at = pl.ds(pl.multiple_of(step * 128, 128), 128)
            spots = [cols[b, n] for n in range(listed)]
            pens = [
                bias[spots[n]] + jnp.where(same[b, n] == 1, 0.0, LOW) for n in range(listed)
            ]
            first = jnp.where(diagonal, 0.0, jnp.broadcast_to(pens[0], (128, 128)))
            for h in range(heads):
                query = qkv[part][h, :, at].astype(F32).T.astype(BF16)
                key_t = jnp.concatenate(
                    [keys[h, :, pl.ds(pl.multiple_of(s * 128, 128), 128)] for s in spots], axis=1
                )
                val = jnp.concatenate(
                    [vals[h, pl.ds(pl.multiple_of(s * 128, 128), 128), :] for s in spots], axis=0
                )
                scores = jnp.dot(query, key_t, preferred_element_type=F32) * SCALE
                scores = jnp.concatenate(
                    [scores[:, :128] + first]
                    + [scores[:, n * 128 : (n + 1) * 128] + pens[n] for n in range(1, listed)],
                    axis=1,
                )
                largest = jnp.max(scores, axis=1, keepdims=True)
                expd = jnp.exp(scores - largest)
                probs = expd * (1.0 / jnp.sum(expd, axis=1, keepdims=True))
                probs = probs.astype(BF16)
                probs_out[h, b] = probs
                att = jnp.dot(probs, val, preferred_element_type=F32)
                att_out[part, h, :, at] = att.T.astype(BF16)


def backward_kernel(parts, heads, count, cols, *refs):
    qkv, d_att = refs[:parts], refs[parts : 2 * parts]
    probs_in = refs[2 * parts]
    out = refs[2 * parts + 1]
    keys, keys_t, vals_t, acc_k, acc_v = refs[2 * parts + 2 :]
    width = qkv[0].shape[2]
    for k in range(parts):
        span = slice(k * width, (k + 1) * width)
        for h in range(heads):
            keys[h, span, :] = qkv[k][heads + h].astype(F32).T.astype(BF16)
            keys_t[h, :, span] = qkv[k][heads + h]
            vals_t[h, :, span] = qkv[k][2 * heads + h]
    acc_k[...] = jnp.zeros_like(acc_k)
    acc_v[...] = jnp.zeros_like(acc_v)
    per = count // parts
    listed = cols.shape[1]
    for part in range(parts):

        @pl.loop(0, per)
        def _(step):
            b = part * per + step
            at = pl.ds(pl.multiple_of(step * 128, 128), 128)
            spots = [
                pl.ds(pl.multiple_of(cols[b, n] * 128, 128), 128) for n in range(listed)
            ]
            for h in range(heads):
                d_t = d_att[part][h, :, at]
                query_t = qkv[part][h, :, at]
                val_t = jnp.concatenate([vals_t[h, :, s] for s in spots], axis=1)
                key = jnp.concatenate([keys[h, s, :] for s in spots], axis=0)
                d_probs = jnp.dot(
                    d_t.astype(F32).T.astype(BF16), val_t, preferred_element_type=F32
                )
                probs_low = probs_in[h, b]
                probs = probs_low.astype(F32)
                weighted = probs * d_probs
                delta = jnp.sum(weighted, axis=1, keepdims=True)
                d_scores = ((weighted - probs * delta) * SCALE).astype(BF16)
                d_query = jnp.dot(d_scores, key, preferred_element_type=F32)
                out[part, h, :, at] = d_query.T.astype(BF16)
                d_key = jnp.dot(query_t, d_scores, preferred_element_type=F32)
                d_val = jnp.dot(d_t, probs_low, preferred_element_type=F32)
                for n in range(listed):
                    acc_k[h, :, spots[n]] += d_key[:, n * 128 : (n + 1) * 128]
                    acc_v[h, :, spots[n]] += d_val[:, n * 128 : (n + 1) * 128]

    for k in range(parts):
        span = slice(k * width, (k + 1) * width)
        for h in range(heads):
            out[k, heads + h] = acc_k[h, :, span].astype(BF16)
            out[k, 2 * heads + h] = acc_v[h, :, span].astype(BF16)


def attend(qkv, cols, same, bias):
    parts, heads = len(qkv), qkv[0].shape[0] // 3
    width = qkv[0].shape[2]
    count, listed = cols.shape
    length = width * parts
    smem = pl.BlockSpec(memory_space=pltpu.SMEM)
    vmem = pl.BlockSpec(memory_space=pltpu.VMEM)
    return pl.pallas_call(
        functools.partial(forward_kernel, parts, heads, count),
        out_shape=(
            jax.ShapeDtypeStruct((parts, heads, HD, width), BF16),
            jax.ShapeDtypeStruct((heads, count, 128, listed * 128), BF16),
        ),
        in_specs=[smem, smem, vmem] + [vmem] * parts,
        out_specs=(vmem, vmem),
        scratch_shapes=[
            pltpu.VMEM((heads, HD, length), BF16),
            pltpu.VMEM((heads, length, HD), BF16),
        ],
        compiler_params=pltpu.CompilerParams(vmem_limit_bytes=40 << 20),
        name="attend",
    )(cols, same, bias, *qkv)


def attend_back(qkv, d_att, probs, cols):
    parts, heads = len(qkv), qkv[0].shape[0] // 3
    width = qkv[0].shape[2]
    count = cols.shape[0]
    length = width * parts
    smem = pl.BlockSpec(memory_space=pltpu.SMEM)
    vmem = pl.BlockSpec(memory_space=pltpu.VMEM)
    return pl.pallas_call(
        functools.partial(backward_kernel, parts, heads, count),
        out_shape=jax.ShapeDtypeStruct((parts, 3 * heads, HD, width), BF16),
        in_specs=[smem] + [vmem] * (2 * parts + 1),
        out_specs=vmem,
        scratch_shapes=[
            pltpu.VMEM((heads, length, HD), BF16),
            pltpu.VMEM((heads, HD, length), BF16),
            pltpu.VMEM((heads, HD, length), BF16),
            pltpu.VMEM((heads, HD, length), F32),
            pltpu.VMEM((heads, HD, length), F32),
        ],
        compiler_params=pltpu.CompilerParams(vmem_limit_bytes=40 << 20),
        name="attend_back",
    )(cols, *qkv, *d_att, probs)


def dot(left, right, axes):
    return lax.dot_general(left, right, (axes, ((), ())), preferred_element_type=F32)


def body(tokens, weights, cotangent, col_list, cut_lengths, keep_mask):
    parts, replicas = lax.axis_size("seq"), lax.axis_size("dp")
    z = lax.axis_index("seq")
    place = z.astype(jnp.int32).reshape(1)
    index = lax.axis_index("dp").astype(jnp.int32).reshape(1)
    inputs, upstream = tokens[0], cotangent[0]
    group = weights.shape[2] // parts
    heads = group // HD
    orders = bit_orders(replicas)

    pieces = chain(inputs)

    low, high = ordered_shard(weights, place, parts)
    low = in_order(gather_shards(low, orders[0] + [1]), index)
    high = in_order(gather_shards(high, orders[1] + [1]), index)
    outer = low[:, 3 * group : (3 + parts) * group]

    columns = col_list[0]
    count = columns.shape[0]
    turn = z * (count // parts)
    columns = jnp.roll((columns - turn) % count, -turn, axis=0)
    ends = jnp.cumsum(cut_lengths[0])
    spots = (jnp.arange(count, dtype=jnp.int32) + turn) % count
    owner = jnp.sum((ends[None, :] <= spots[:, None]).astype(jnp.int32), axis=1)
    same = (owner[columns] == owner[:, None]).astype(jnp.int32)
    bias = jnp.where(jnp.roll(keep_mask[0].reshape(count, 1, -1), -turn, axis=0) == 1, 0.0, LOW)

    d_all = dot(outer, upstream, ((0,), (1,))).astype(BF16)
    d_own = [d_all[k * group : (k + 1) * group] for k in range(parts)]
    d_att = [d_own[0]] + [shifted(d_own[parts - k], parts - k) for k in range(1, parts)]
    d_att = [d.reshape(heads, HD, -1) for d in d_att]

    own_inner = low[:, : 3 * group]
    qkv = [
        dot(own_inner, piece, ((0,), (1,))).astype(BF16).reshape(3 * heads, HD, -1)
        for piece in pieces
    ]
    att, probs = attend(qkv, columns, same, bias)
    att = att.reshape(parts, group, -1)
    att_here = [att[0]] + [shifted(att[parts - j], parts - j) for j in range(1, parts)]
    att_here = jnp.concatenate(att_here, axis=0)
    result = dot(att_here, outer, ((0,), (1,))).astype(BF16)
    outer_sum = scatter_rows(
        *gradient_halves([att_here], [upstream], index, replicas), orders
    )

    d_qkv = attend_back(qkv, d_att, probs, columns)
    d_qkv = d_qkv.reshape(parts, 3 * group, -1)
    inner_sum = scatter_rows(
        *gradient_halves([d_qkv[k] for k in range(parts)], pieces, index, replicas), orders
    )
    d_here = [d_qkv[0]] + [shifted(d_qkv[parts - j], parts - j) for j in range(1, parts)]
    d_here = jnp.concatenate(d_here, axis=0)
    grad_in = dot(
        d_here[: 3 * group], own_inner, ((0,), (1,))
    ) + dot(
        d_here[3 * group :],
        jnp.concatenate([low[:, (3 + parts) * group :], high], axis=1),
        ((0,), (1,)),
    )
    grad_in = grad_in.astype(BF16)

    outer_low = outer_sum.astype(BF16)
    outer_own = outer_sum[:, :group]
    for j in range(1, parts):
        outer_own = outer_own + shifted(
            outer_low[:, j * group : (j + 1) * group], j
        ).astype(F32)
    own = jnp.concatenate([inner_sum, outer_own], axis=1).astype(BF16)
    found = [own] + [shifted(own, parts - j) for j in range(1, parts)]
    grad_all = final_rows(found, place, replicas)
    return (result[None], grad_in[None], grad_all)


def solution(mesh):
    placed = (
        P("dp", "seq", None),
        P("dp", None, None),
        P("dp", "seq", None),
        P("dp", None, None),
        P("dp", None),
        P("dp", None),
    )
    return jax.shard_map(
        body,
        mesh=mesh,
        in_specs=placed,
        out_specs=(P("dp", "seq", None), P("dp", "seq", None), P("dp", None, None)),
        check_vma=False,
    )
```

```python
import functools
import math

import jax
import jax.numpy as jnp
from jax import lax
from jax.experimental import pallas as pl
from jax.experimental.pallas import tpu as pltpu
from jax.sharding import PartitionSpec as P

HD = 88
SCALE = 1.0 / math.sqrt(HD)
LOW = -1e30
F32 = jnp.float32
BF16 = jnp.bfloat16


def shifted(array, step):
    count = lax.axis_size("seq")
    return lax.ppermute(array, "seq", [(i, (i + step) % count) for i in range(count)])


def exchanged(array, bit):
    count = lax.axis_size("dp")
    return lax.ppermute(array, "dp", [(i, i ^ bit) for i in range(count)])


def bit_orders(count):
    far = [1 << i for i in range(1, count.bit_length() - 1)]
    half = len(far) // 2
    return far, far[half:] + far[:half]


def block_order(bits):
    if not bits:
        return [0]
    rest = block_order(bits[1:])
    return [r | bits[0] for r in rest] + rest


VMEM = pl.BlockSpec(memory_space=pltpu.VMEM)
SMEM = pl.BlockSpec(memory_space=pltpu.SMEM)


def call(kernel, out_shape, scratch, name, scalars, arrays, flops=1):
    single = not isinstance(out_shape, tuple)
    return pl.pallas_call(
        kernel,
        out_shape=out_shape,
        in_specs=[SMEM] * len(scalars) + [VMEM] * len(arrays),
        out_specs=VMEM if single else (VMEM,) * len(out_shape),
        scratch_shapes=scratch,
        compiler_params=pltpu.CompilerParams(vmem_limit_bytes=24 << 20),
        cost_estimate=pl.CostEstimate(flops=flops, bytes_accessed=1, transcendentals=0),
        name=name,
    )(*scalars, *arrays)


def together(*trees):
    return lax.optimization_barrier(trees)


def shape_of(*dims, dtype=BF16):
    return jax.ShapeDtypeStruct(dims, dtype)


def far_indices(orders):
    return sorted(range(0, 2 << len(orders[0]), 2), key=lambda r: (bin(r).count("1"), r))


def parting_kernel(spans, *refs):
    count = len(spans)
    for span, piece, out in zip(spans, refs[:count], refs[count:]):
        out[...] = piece[:, span]


def passed_on(held, several, orders):
    for r in several:
        last = [max((b for b in order if b & r), key=order.index) for order in orders]
        parts = []
        for n in range(2):
            source = held[r ^ last[n]]
            half = source[0].shape[1] // 2
            parts.append(
                (source[n], slice(None)) if len(source) == 2
                else (source[0], slice(n * half, (n + 1) * half))
            )
        rows = parts[0][0].shape[0]
        half = held[0][0].shape[1] // 2
        parts = call(
            functools.partial(parting_kernel, [span for _, span in parts]),
            (shape_of(rows, half),) * 2, [], "parting", [], [piece for piece, _ in parts],
            flops=1 << 36,
        )
        held[r] = [exchanged(parts[n], last[n]) for n in range(2)]


def in_order_kernel(sizes, index, *refs):
    pieces, out, at = refs[:-1], refs[-1], 0
    half = out.shape[2] // 2
    for r, size in sizes:
        if size == 1:
            out[index[0] ^ r] = pieces[at][...]
        else:
            out[index[0] ^ r, :, :half] = pieces[at][...]
            out[index[0] ^ r, :, half:] = pieces[at + 1][...]
        at += size


def in_order(held, index):
    count, (rows, columns) = len(held), held[0][0].shape
    out = call(
        functools.partial(in_order_kernel, [(r, len(held[r])) for r in held]),
        shape_of(count, rows, columns), [], "in_order", [index],
        [piece for r in held for piece in held[r]],
    )
    return out.reshape(count * rows, columns)


def mark_kernel(one, other, out):
    out[...] = one[...] + other[...]


def shard_kernel(parts, place, weights, low, high):
    group = weights.shape[2] // parts
    for z in range(parts):

        @pl.when(place[0] == z)
        def _():
            cols = [weights[:, c, :] for c in range(4)]

            def block(c, j):
                start = (z + j) % parts * group
                return cols[c][:, start : start + group]

            chosen = [block(c, 0) for c in range(3)] + [block(3, j) for j in range(parts)]
            chosen += [block(c, j) for j in range(1, parts) for c in range(3)]
            low[...] = jnp.concatenate(chosen[: 2 * parts], axis=1)
            high[...] = jnp.concatenate(chosen[2 * parts :], axis=1)


def project_kernel(parts, group, rows, low, *out):
    outer = low[:, 3 * group : (3 + parts) * group]
    total = jnp.dot(rows[...], outer, preferred_element_type=F32).T
    for j in range(parts):
        out[j][...] = total[j * group : (j + 1) * group].astype(BF16)


def result_kernel(parts, group, low, *refs):
    att, (out, scratch) = refs[:parts], refs[parts:]
    for j in range(parts):
        scratch[j * group : (j + 1) * group, :] = att[j][...].astype(F32)
    left = scratch[...].T.astype(BF16)
    outer = low[:, 3 * group : (3 + parts) * group]
    out[...] = lax.dot_general(
        left, outer, (((1,), (1,)), ((), ())), preferred_element_type=F32
    ).astype(BF16)


def grad_in_kernel(parts, group, low, high, *refs):
    d_here, (out, scratch) = refs[:parts], refs[parts:]
    for j in range(parts):
        scratch[j * 3 * group : (j + 1) * 3 * group, :] = d_here[j][...].astype(F32)
    left = scratch[...].T.astype(BF16)
    first, rest = 3 * group, left.shape[1] - high.shape[1]
    contract = (((1,), (1,)), ((), ()))
    total = lax.dot_general(
        left[:, rest:], high[...], contract, preferred_element_type=F32
    )
    total += lax.dot_general(
        left[:, :first], low[:, :first], contract, preferred_element_type=F32
    )
    if rest > first:
        total += lax.dot_general(
            left[:, first:rest], low[:, (3 + parts) * group :], contract,
            preferred_element_type=F32,
        )
    out[...] = total.astype(BF16)


def store_rows(whole, start, value):
    rows, end = whole.shape[1], start + value.shape[0]
    at = start
    while at < end:
        block, first = divmod(at, rows)
        size = min(rows - first, end - at)
        whole[block, first : first + size, :] = value[at - start : at - start + size]
        at += size


def emit_halves(index, whole, order, sent, kept):
    for i, r in enumerate(block_order(order)):
        mine = index[0] ^ r
        kept[i] = whole[mine]
        sent[i] = whole[mine ^ 1].astype(BF16)


def outer_gradient_kernel(parts, order, index, rows, *refs):
    att, (sent, kept, whole) = refs[:parts], refs[parts:]
    left = jnp.concatenate([a[...] for a in att], axis=0)
    for start in range(0, rows.shape[1], 128):
        span = slice(start, start + 128)
        store_rows(whole, start, jnp.dot(left, rows[:, span], preferred_element_type=F32).T)
    emit_halves(index, whole, order, sent, kept)


def gradient_halves(kernel, name, columns, scalars, arrays, replicas):
    width = arrays[0].shape[-1]
    shape = (replicas // 2, width // replicas, columns)
    return call(
        kernel, (shape_of(*shape), shape_of(*shape, dtype=F32)),
        [pltpu.VMEM((replicas, width // replicas, columns), F32)], name, scalars, arrays, flops=1 << 34,
    )


def combine_kernel(cut, inner, inner_more, outer, outer_more, kept, *out):
    count = inner.shape[0]
    for i in range(count):
        left = inner[i] + inner_more[i].astype(F32)
        right = outer[i] + outer_more[i].astype(F32)
        if i < count - 1:
            out[i][:, :cut] = left.astype(BF16)
            out[i][:, cut:] = right.astype(BF16)
        else:
            kept[:, :cut] = left
            kept[:, cut:] = right


def finish_kernel(cut, group, kept, *refs):
    parts = (kept.shape[1] - cut) // group
    arrived, (inner, *outer) = refs[: -parts - 1], refs[-parts - 1 :]
    total = kept[...]
    for more in arrived:
        total += more[...].astype(F32)
    inner[...] = total[:, :cut].astype(BF16)
    for j in range(parts):
        outer[j][...] = total[:, cut + j * group : cut + (j + 1) * group].astype(BF16)


def own_kernel(inner, *refs):
    pieces, out = refs[:-1], refs[-1]
    cut = inner.shape[1]
    out[:, :cut] = inner[...]
    total = pieces[0][...].astype(F32)
    for piece in pieces[1:]:
        total += piece[...].astype(F32)
    out[:, cut:] = total.astype(BF16)


def final_kernel(parts, replicas, place, *refs):
    found, out = refs[:-1], refs[-1]
    group = out.shape[2] // parts
    for z in range(parts):

        @pl.when(place[0] == z)
        def _():
            turn = [(hg - z) % parts for hg in range(parts)]
            for c in range(4):
                span = slice(c * group, (c + 1) * group)
                out[:, c, :] = jnp.concatenate(
                    [found[j][:, span].astype(F32) for j in turn], axis=1
                ) * (1.0 / replicas)


def hop(ups, downs):
    count, done = lax.axis_size("seq"), len(ups)
    down = lax.ppermute(downs[-1], "seq", [(i, i + 1) for i in range(done - 1, count - 1)])
    up = lax.ppermute(ups[-1], "seq", [(i, i - 1) for i in range(1, count - done + 1)])
    return ups + [up], downs + [down]


def store_projection(qkv, k, rows, own):
    total = jnp.dot(rows[...], own, preferred_element_type=F32).T
    for i in range(qkv.shape[1]):
        qkv[k, i] = total[i * HD : (i + 1) * HD].astype(BF16)


def early_kernel(parts, place, low, *refs):
    ups, downs = refs[: parts - 1], refs[parts - 1 : 2 * parts - 3]
    rows, qkv = refs[2 * parts - 3 :]
    own = low[:, : qkv.shape[1] * HD]
    rows[0] = ups[0][...]
    for k in range(1, parts):
        if k < parts - 1:

            @pl.when(place[0] + k < parts)
            def _():
                rows[k] = ups[k][...]

        if parts - k < parts - 1:

            @pl.when(place[0] + k >= parts)
            def _():
                rows[k] = downs[parts - k - 1][...]

    for k in range(parts):
        store_projection(qkv, k, rows.at[k], own)


def forward_kernel(parts, heads, cols, same, place, bias, low, up, down, early, *refs):
    qkv, att_out = refs[0], refs[1 : parts + 1]
    probs_out, keys, vals = refs[parts + 1 :]
    group, width = heads * HD, qkv.shape[3]
    qkv[...] = early[...]
    own = low[:, : 3 * group]

    @pl.when(place[0] == 0)
    def _():
        store_projection(qkv, parts - 1, up, own)

    @pl.when(place[0] == parts - 1)
    def _():
        store_projection(qkv, 1, down, own)

    for k in range(parts):
        span = slice(k * width, (k + 1) * width)
        for h in range(heads):
            keys[h, :, span] = qkv[k, heads + h]
            vals[h, span, :] = qkv[k, 2 * heads + h].astype(F32).T.astype(BF16)
    count, listed = cols.shape
    per = count // parts
    line = lax.broadcasted_iota(jnp.int32, (128, 128), 0)
    lanes = lax.broadcasted_iota(jnp.int32, (128, 128), 1)
    diagonal = line == lanes
    for part in range(parts):

        for step in range(per):
            b = part * per + step
            at = slice(step * 128, (step + 1) * 128)
            spots = [cols[b, n] for n in range(listed)]
            pens = [
                bias[spots[n]] + jnp.where(same[b, n] == 1, 0.0, LOW) for n in range(listed)
            ]
            first = jnp.where(diagonal, 0.0, jnp.broadcast_to(pens[0], (128, 128)))
            for h in range(heads):
                query = qkv[part, h, :, at].astype(F32).T.astype(BF16)
                key_t = jnp.concatenate(
                    [keys[h, :, pl.ds(pl.multiple_of(s * 128, 128), 128)] for s in spots], axis=1
                )
                val = jnp.concatenate(
                    [vals[h, pl.ds(pl.multiple_of(s * 128, 128), 128), :] for s in spots], axis=0
                )
                scores = jnp.dot(query, key_t, preferred_element_type=F32) * SCALE
                scores = jnp.concatenate(
                    [scores[:, :128] + first]
                    + [scores[:, n * 128 : (n + 1) * 128] + pens[n] for n in range(1, listed)],
                    axis=1,
                )
                largest = jnp.max(scores, axis=1, keepdims=True)
                expd = jnp.exp(scores - largest)
                probs = expd * (1.0 / jnp.sum(expd, axis=1, keepdims=True))
                probs = probs.astype(BF16)
                probs_out[h, b] = probs
                att = jnp.dot(probs, val, preferred_element_type=F32)
                att_out[part][h, :, at] = att.T.astype(BF16)


def backward_kernel(parts, heads, order, cols, place, index, qkv, probs_in, rows, up, down, *refs):
    d_att, out = refs[:parts], refs[parts : 2 * parts]
    sent, kept, keys, keys_t, vals_t, acc, whole = refs[2 * parts :]
    width = qkv.shape[3]
    group = heads * HD
    for k in range(parts):
        span = slice(k * width, (k + 1) * width)
        for h in range(heads):
            keys[h, span, :] = qkv[k, heads + h].astype(F32).T.astype(BF16)
            keys_t[h, :, span] = qkv[k, heads + h]
            vals_t[h, :, span] = qkv[k, 2 * heads + h]
    acc[group:, :] = jnp.zeros_like(acc[group:, :])
    count, listed = cols.shape
    per = count // parts
    for part in range(parts):

        for step in range(per):
            b = part * per + step
            at = slice(step * 128, (step + 1) * 128)
            into = slice(b * 128, (b + 1) * 128)
            spots = [
                pl.ds(pl.multiple_of(cols[b, n] * 128, 128), 128) for n in range(listed)
            ]
            for h in range(heads):
                d_t = d_att[part][h, :, at]
                query_t = qkv[part, h, :, at]
                val_t = jnp.concatenate([vals_t[h, :, s] for s in spots], axis=1)
                key = jnp.concatenate([keys[h, s, :] for s in spots], axis=0)
                d_probs = jnp.dot(
                    d_t.astype(F32).T.astype(BF16), val_t, preferred_element_type=F32
                )
                probs_low = probs_in[h, b]
                probs = probs_low.astype(F32)
                weighted = probs * d_probs
                delta = jnp.sum(weighted, axis=1, keepdims=True)
                d_scores = ((weighted - probs * delta) * SCALE).astype(BF16)
                d_query = jnp.dot(d_scores, key, preferred_element_type=F32)
                acc[h * HD : (h + 1) * HD, into] = d_query.T
                d_key = jnp.dot(query_t, d_scores, preferred_element_type=F32)
                d_val = jnp.dot(d_t, probs_low, preferred_element_type=F32)
                for n in range(listed):
                    block = slice(n * 128, (n + 1) * 128)
                    acc[(heads + h) * HD : (heads + h + 1) * HD, spots[n]] += d_key[:, block]
                    acc[(2 * heads + h) * HD : (2 * heads + h + 1) * HD, spots[n]] += d_val[:, block]

    left = acc[...].astype(BF16)
    for k in range(parts):
        out[k][...] = left[:, k * width : (k + 1) * width]
    for start in range(0, rows.shape[2], 128):
        span = slice(start, start + 128)
        pieces = [rows[k, :, span] for k in range(parts)]
        pieces[parts - 1] = jnp.where(place[0] == 0, up[:, span], pieces[parts - 1])
        pieces[1] = jnp.where(place[0] == parts - 1, down[:, span], pieces[1])
        right = jnp.concatenate(pieces, axis=0)
        store_rows(whole, start, jnp.dot(left, right, preferred_element_type=F32).T)
    emit_halves(index, whole, order, sent, kept)


def traded(pieces):
    count = len(pieces)
    return [pieces[0]] + [shifted(pieces[count - j], count - j) for j in range(1, count)]


def body(tokens, weights, cotangent, col_list, cut_lengths, keep_mask):
    parts, replicas = lax.axis_size("seq"), lax.axis_size("dp")
    z = lax.axis_index("seq")
    place = z.astype(jnp.int32).reshape(1)
    index = lax.axis_index("dp").astype(jnp.int32).reshape(1)
    inputs, upstream = tokens[0], cotangent[0]
    width, model = inputs.shape
    shard, _, wide = weights.shape
    group = wide // parts
    heads = group // HD
    orders = bit_orders(replicas)
    length = parts * width

    columns = col_list[0]
    count, listed = columns.shape
    turn = z * (count // parts)
    columns = jnp.roll((columns - turn) % count, -turn, axis=0)
    ends = jnp.cumsum(cut_lengths[0])
    spots = (jnp.arange(count, dtype=jnp.int32) + turn) % count
    owner = jnp.sum((ends[None, :] <= spots[:, None]).astype(jnp.int32), axis=1)
    same = (owner[columns] == owner[:, None]).astype(jnp.int32)
    bias = jnp.where(jnp.roll(keep_mask[0].reshape(count, 1, -1), -turn, axis=0) == 1, 0.0, LOW)

    low, high = call(
        functools.partial(shard_kernel, parts), (shape_of(shard, 2 * wide),) * 2, [],
        "ordered_shard", [place], [weights],
    )

    far = far_indices(orders)
    single = [r for r in far if bin(r).count("1") == 1]
    several = [r for r in far if bin(r).count("1") > 1]
    ups, downs = hop([inputs], [inputs])
    mark = call(
        mark_kernel, shape_of(8, 128), [], "mark", [], [ups[1][:8, :128], downs[1][:8, :128]],
        flops=1 << 36,
    )
    lows = {r: [exchanged(low, r)] for r in single}
    ups, downs, lows, mark = together(ups, downs, lows, mark)

    while len(ups) < parts - 1:
        ups, downs = hop(ups, downs)
    lows[0] = [low]
    passed_on(lows, several, orders)
    for r in far:
        lows[r | 1] = [exchanged(piece, 1) for piece in lows[r]]
    mark = call(
        mark_kernel, shape_of(8, 128), [], "mark", [], [ups[-1][:8, :128], downs[-1][:8, :128]],
        flops=1 << 36,
    )
    ups, downs, lows, high, mark = together(ups, downs, lows, high, mark)

    ups, downs = hop(ups, downs)
    highs = {r: [exchanged(high, r)] for r in single}
    highs[0] = [high]
    passed_on(highs, several, orders)
    low = in_order(lows, index)
    d_att = call(
        functools.partial(project_kernel, parts, group),
        (shape_of(group, width),) * parts, [], "project", [], [upstream, low],
    )
    rows, early = call(
        functools.partial(early_kernel, parts),
        (shape_of(parts, width, model), shape_of(parts, 3 * heads, HD, width)),
        [], "early", [place], [low] + ups[:-1] + downs[1:-1], flops=1 << 33,
    )
    ups, downs, d_att, rows, early, highs = together(ups, downs, d_att, rows, early, highs)

    d_att = [d.reshape(heads, HD, width) for d in traded(d_att)]
    results = call(
        functools.partial(forward_kernel, parts, heads),
        (shape_of(parts, 3 * heads, HD, width),)
        + (shape_of(heads, HD, width),) * parts
        + (shape_of(heads, count, 128, listed * 128),),
        [pltpu.VMEM((heads, HD, length), BF16), pltpu.VMEM((heads, length, HD), BF16)],
        "attend", [columns, same, place], [bias, low, ups[-1], downs[-1], early],
        flops=1 << 34,
    )
    d_att, results, highs = together(d_att, results, highs)
    qkv, att, probs = results[0], results[1:-1], results[-1]

    att = traded([a.reshape(group, width) for a in att])
    halved = (replicas // 2, shard, 3 * group)
    back = call(
        functools.partial(backward_kernel, parts, heads, orders[0]),
        (shape_of(3 * group, width),) * parts + (shape_of(*halved), shape_of(*halved, dtype=F32)),
        [
            pltpu.VMEM((heads, length, HD), BF16),
            pltpu.VMEM((heads, HD, length), BF16),
            pltpu.VMEM((heads, HD, length), BF16),
            pltpu.VMEM((3 * group, length), F32),
            pltpu.VMEM((replicas, shard, 3 * group), F32),
        ],
        "attend_back", [columns, place, index],
        [qkv, probs, rows, ups[-1], downs[-1]] + list(d_att), flops=1 << 34,
    )
    att, back, highs = together(att, back, highs)
    for r in far:
        highs[r | 1] = [exchanged(piece, 1) for piece in highs[r]]

    d_qkv, sent, inner_sum = back[:parts], back[parts], back[parts + 1]
    d_here = [d_qkv[0]] + [None] * (parts - 1)
    def fetch(which):
        for j in which:
            d_here[j] = shifted(d_qkv[parts - j], parts - j)

    fetch([1, parts - 1])
    inner_more = exchanged(sent, 1)
    sent, outer_sum = gradient_halves(
        functools.partial(outer_gradient_kernel, parts, orders[0]), "outer_gradient", wide,
        [index], [upstream] + list(att), replicas,
    )
    outer_more = exchanged(sent, 1)
    cut = 3 * group
    away = block_order(orders[0])[:-1]
    kept, *given = call(
        functools.partial(combine_kernel, cut),
        (shape_of(shard, cut + wide, dtype=F32),) + (shape_of(shard, cut + wide),) * len(away),
        [], "combine", [], [inner_sum, inner_more, outer_sum, outer_more], flops=1 << 33,
    )
    arrived = [exchanged(piece, r) for piece, r in zip(given, away)]
    d_qkv, d_here[1] = together(d_qkv, d_here[1])
    fetch(range(2, parts - 1))
    inner_own, *pieces = call(
        functools.partial(finish_kernel, cut, group),
        (shape_of(shard, cut),) + (shape_of(shard, group),) * parts,
        [], "finish", [], [kept] + arrived,
    )
    pieces, d_here = together(pieces, d_here)

    own = call(own_kernel, shape_of(shard, cut + group), [], "own", [], [inner_own] + traded(pieces))
    own, att = together(own, att)
    found = [own] + [shifted(own, parts - j) for j in range(1, parts)]
    result = call(
        functools.partial(result_kernel, parts, group),
        shape_of(width, model), [pltpu.VMEM((wide, width), F32)], "result", [],
        [low] + list(att), flops=1 << 32,
    )
    high = in_order(highs, index)
    grad_in = call(
        functools.partial(grad_in_kernel, parts, group),
        shape_of(width, model), [pltpu.VMEM((3 * wide, width), F32)],
        "grad_in", [], [low, high] + list(d_here), flops=1 << 33,
    )
    grad_all = call(
        functools.partial(final_kernel, parts, replicas),
        shape_of(shard, 4, wide, dtype=F32), [], "final_rows", [place], found,
    )
    return (result[None], grad_in[None], grad_all)


def solution(mesh):
    placed = (
        P("dp", "seq", None),
        P("dp", None, None),
        P("dp", "seq", None),
        P("dp", None, None),
        P("dp", None),
        P("dp", None),
    )
    return jax.shard_map(
        body,
        mesh=mesh,
        in_specs=placed,
        out_specs=(P("dp", "seq", None), P("dp", "seq", None), P("dp", None, None)),
        check_vma=False,
    )
```

```python
import functools
import math

import jax
import jax.numpy as jnp
from jax import lax
from jax.experimental import pallas as pl
from jax.experimental.pallas import tpu as pltpu
from jax.sharding import PartitionSpec as P

HD = 88
SCALE = 1.0 / math.sqrt(HD)
LOW = -1e30
F32 = jnp.float32
BF16 = jnp.bfloat16


def shifted(array, step):
    count = lax.axis_size("seq")
    return lax.ppermute(array, "seq", [(i, (i + step) % count) for i in range(count)])


def exchanged(array, bit):
    count = lax.axis_size("dp")
    return lax.ppermute(array, "dp", [(i, i ^ bit) for i in range(count)])


def bit_orders(count):
    far = [1 << i for i in range(1, count.bit_length() - 1)]
    half = len(far) // 2
    return far, far[half:] + far[:half]


def block_order(bits):
    if not bits:
        return [0]
    rest = block_order(bits[1:])
    return [r | bits[0] for r in rest] + rest


VMEM = pl.BlockSpec(memory_space=pltpu.VMEM)
SMEM = pl.BlockSpec(memory_space=pltpu.SMEM)


def call(kernel, out_shape, scratch, name, scalars, arrays, flops=1, limit=16):
    single = not isinstance(out_shape, tuple)
    return pl.pallas_call(
        kernel,
        out_shape=out_shape,
        in_specs=[SMEM] * len(scalars) + [VMEM] * len(arrays),
        out_specs=VMEM if single else (VMEM,) * len(out_shape),
        scratch_shapes=scratch,
        compiler_params=pltpu.CompilerParams(vmem_limit_bytes=limit << 20),
        cost_estimate=pl.CostEstimate(flops=flops, bytes_accessed=1, transcendentals=0),
        name=name,
    )(*scalars, *arrays)


def together(*trees):
    return lax.optimization_barrier(trees)


def shape_of(*dims, dtype=BF16):
    return jax.ShapeDtypeStruct(dims, dtype)


def far_indices(orders):
    return sorted(range(0, 2 << len(orders[0]), 2), key=lambda r: (bin(r).count("1"), r))


def parting_kernel(spans, *refs):
    count = len(spans)
    for span, piece, out in zip(spans, refs[:count], refs[count:]):
        out[...] = piece[:, span]


def parted_for(held, r, orders):
    half = held[0][0].shape[1] // 2
    parts = []
    for n, order in enumerate(orders):
        source = held.get(r ^ max((b for b in order if b & r), key=order.index))
        if source is None:
            return None
        whole = len(source) == 1
        parts.append((source[0], slice(n * half, (n + 1) * half)) if whole else (source[n], slice(None)))
    return call(
        functools.partial(parting_kernel, [span for _, span in parts]),
        (shape_of(parts[0][0].shape[0], half),) * 2, [], "parting", [],
        [piece for piece, _ in parts],
    )


def passed_on(held, several, parted, orders):
    for r, halves in zip(several, parted):
        halves = halves or parted_for(held, r, orders)
        last = [max((b for b in order if b & r), key=order.index) for order in orders]
        held[r] = [exchanged(halves[n], last[n]) for n in range(2)]


def in_order_kernel(sizes, index, *refs):
    pieces, out, at = refs[:-1], refs[-1], 0
    half = out.shape[2] // 2
    for r, size in sizes:
        if size == 1:
            out[index[0] ^ r] = pieces[at][...]
        else:
            out[index[0] ^ r, :, :half] = pieces[at][...]
            out[index[0] ^ r, :, half:] = pieces[at + 1][...]
        at += size


def in_order(held, index, flops=1):
    count, (rows, columns) = len(held), held[0][0].shape
    out = call(
        functools.partial(in_order_kernel, [(r, len(held[r])) for r in held]),
        shape_of(count, rows, columns), [], "in_order", [index],
        [piece for r in held for piece in held[r]], flops=flops,
    )
    return out.reshape(count * rows, columns)


def mark_kernel(piece, out):
    out[...] = piece[...]


def shard_kernel(parts, place, weights, low, high):
    group = weights.shape[2] // parts
    for z in range(parts):

        @pl.when(place[0] == z)
        def _():
            cols = [weights[:, c, :] for c in range(4)]

            def block(c, j):
                start = (z + j) % parts * group
                return cols[c][:, start : start + group]

            chosen = [block(c, 0) for c in range(3)] + [block(3, j) for j in range(parts)]
            chosen += [block(c, j) for j in range(1, parts) for c in range(3)]
            low[...] = jnp.concatenate(chosen[: 2 * parts], axis=1)
            high[...] = jnp.concatenate(chosen[2 * parts :], axis=1)


def project_kernel(parts, group, rows, low, *out):
    outer = low[:, 3 * group : (3 + parts) * group]
    total = jnp.dot(rows[...], outer, preferred_element_type=F32).T
    for j in range(parts):
        out[j][...] = total[j * group : (j + 1) * group].astype(BF16)


def result_kernel(parts, group, low, *refs):
    att, (out, scratch) = refs[:parts], refs[parts:]
    for j in range(parts):
        scratch[j * group : (j + 1) * group, :] = att[j][...].astype(F32)
    left = scratch[...].T.astype(BF16)
    outer = low[:, 3 * group : (3 + parts) * group]
    out[...] = lax.dot_general(
        left, outer, (((1,), (1,)), ((), ())), preferred_element_type=F32
    ).astype(BF16)


def grad_in_kernel(parts, group, low, high, *refs):
    d_here, (out, scratch) = refs[:parts], refs[parts:]
    for j in range(parts):
        scratch[j * 3 * group : (j + 1) * 3 * group, :] = d_here[j][...].astype(F32)
    left = scratch[...].T.astype(BF16)
    first, rest = 3 * group, left.shape[1] - high.shape[1]
    contract = (((1,), (1,)), ((), ()))
    total = lax.dot_general(
        left[:, rest:], high[...], contract, preferred_element_type=F32
    )
    total += lax.dot_general(
        left[:, :first], low[:, :first], contract, preferred_element_type=F32
    )
    if rest > first:
        total += lax.dot_general(
            left[:, first:rest], low[:, (3 + parts) * group :], contract,
            preferred_element_type=F32,
        )
    out[...] = total.astype(BF16)


def store_rows(whole, start, value):
    rows, end = whole.shape[1], start + value.shape[0]
    at = start
    while at < end:
        block, first = divmod(at, rows)
        size = min(rows - first, end - at)
        whole[block, first : first + size, :] = value[at - start : at - start + size]
        at += size


def emit_halves(index, whole, order, sent, kept):
    for i, r in enumerate(block_order(order)):
        mine = index[0] ^ r
        kept[i] = whole[mine]
        sent[i] = whole[mine ^ 1].astype(BF16)


def outer_gradient_kernel(parts, order, index, rows, *refs):
    att, (sent, kept, whole) = refs[:parts], refs[parts:]
    left = jnp.concatenate([a[...] for a in att], axis=0)
    for start in range(0, rows.shape[1], 256):
        span = slice(start, min(start + 256, rows.shape[1]))
        store_rows(whole, start, jnp.dot(left, rows[:, span], preferred_element_type=F32).T)
    emit_halves(index, whole, order, sent, kept)


def gradient_halves(kernel, name, columns, scalars, arrays, replicas):
    width = arrays[0].shape[-1]
    shape = (replicas // 2, width // replicas, columns)
    return call(
        kernel, (shape_of(*shape), shape_of(*shape, dtype=F32)),
        [pltpu.VMEM((replicas, width // replicas, columns), F32)], name, scalars, arrays, flops=1 << 34,
    )


def combine_kernel(cut, inner, inner_more, outer, outer_more, kept, *out):
    count = inner.shape[0]
    for i in range(count):
        left = inner[i] + inner_more[i].astype(F32)
        right = outer[i] + outer_more[i].astype(F32)
        if i < count - 1:
            out[i][:, :cut] = left.astype(BF16)
            out[i][:, cut:] = right.astype(BF16)
        else:
            kept[:, :cut] = left
            kept[:, cut:] = right


def finish_kernel(cut, group, kept, *refs):
    parts = (kept.shape[1] - cut) // group
    arrived, (inner, *outer) = refs[: -parts - 1], refs[-parts - 1 :]
    total = kept[...]
    for more in arrived:
        total += more[...].astype(F32)
    inner[...] = total[:, :cut].astype(BF16)
    for j in range(parts):
        outer[j][...] = total[:, cut + j * group : cut + (j + 1) * group].astype(BF16)


def own_kernel(inner, *refs):
    pieces, out = refs[:-1], refs[-1]
    cut = inner.shape[1]
    out[:, :cut] = inner[...]
    total = pieces[0][...].astype(F32)
    for piece in pieces[1:]:
        total += piece[...].astype(F32)
    out[:, cut:] = total.astype(BF16)


def final_kernel(parts, replicas, place, *refs):
    found, out = refs[:-1], refs[-1]
    group = out.shape[2] // parts
    for z in range(parts):

        @pl.when(place[0] == z)
        def _():
            turn = [(hg - z) % parts for hg in range(parts)]
            for c in range(4):
                span = slice(c * group, (c + 1) * group)
                out[:, c, :] = jnp.concatenate(
                    [found[j][:, span].astype(F32) for j in turn], axis=1
                ) * (1.0 / replicas)


def hop(pieces):
    return pieces + [shifted(pieces[-1], -1)]


def store_projection(qkv, k, rows, own):
    total = jnp.dot(rows[...], own, preferred_element_type=F32).T
    for i in range(qkv.shape[1]):
        qkv[k, i] = total[i * HD : (i + 1) * HD].astype(BF16)


def early_kernel(parts, low, *refs):
    pieces, qkv = refs[: parts - 1], refs[-1]
    own = low[:, : qkv.shape[1] * HD]
    for k in range(parts - 1):
        store_projection(qkv, k, pieces[k], own)


def forward_kernel(parts, heads, cols, same, bias, low, piece, early, *refs):
    qkv, att_out = refs[0], refs[1 : parts + 1]
    probs_out, keys, vals = refs[parts + 1 :]
    group, width = heads * HD, qkv.shape[3]
    for k in range(parts - 1):
        qkv[k] = early[k]
    store_projection(qkv, parts - 1, piece, low[:, : 3 * group])
    for k in range(parts):
        span = slice(k * width, (k + 1) * width)
        for h in range(heads):
            keys[h, :, span] = qkv[k, heads + h]
            vals[h, span, :] = qkv[k, 2 * heads + h].astype(F32).T.astype(BF16)
    count, listed = cols.shape
    per = count // parts
    line = lax.broadcasted_iota(jnp.int32, (128, 128), 0)
    lanes = lax.broadcasted_iota(jnp.int32, (128, 128), 1)
    diagonal = line == lanes
    for part in range(parts):

        for step in range(per):
            b = part * per + step
            at = slice(step * 128, (step + 1) * 128)
            spots = [cols[b, n] for n in range(listed)]
            pens = [
                bias[spots[n]] + jnp.where(same[b, n] == 1, 0.0, LOW) for n in range(listed)
            ]
            first = jnp.where(diagonal, 0.0, jnp.broadcast_to(pens[0], (128, 128)))
            for h in range(heads):
                query = qkv[part, h, :, at].astype(F32).T.astype(BF16)
                key_t = jnp.concatenate(
                    [keys[h, :, pl.ds(pl.multiple_of(s * 128, 128), 128)] for s in spots], axis=1
                )
                val = jnp.concatenate(
                    [vals[h, pl.ds(pl.multiple_of(s * 128, 128), 128), :] for s in spots], axis=0
                )
                scores = jnp.dot(query, key_t, preferred_element_type=F32) * SCALE
                scores = jnp.concatenate(
                    [scores[:, :128] + first]
                    + [scores[:, n * 128 : (n + 1) * 128] + pens[n] for n in range(1, listed)],
                    axis=1,
                )
                largest = jnp.max(scores, axis=1, keepdims=True)
                expd = jnp.exp(scores - largest)
                probs = expd * (1.0 / jnp.sum(expd, axis=1, keepdims=True))
                probs = probs.astype(BF16)
                probs_out[h, b] = probs
                att = jnp.dot(probs, val, preferred_element_type=F32)
                att_out[part][h, :, at] = att.T.astype(BF16)


def backward_kernel(parts, heads, order, cols, index, qkv, probs_in, *refs):
    rows, d_att, out = refs[:parts], refs[parts : 2 * parts], refs[2 * parts : 3 * parts]
    sent, kept, keys, keys_t, vals_t, acc, whole = refs[3 * parts :]
    width = qkv.shape[3]
    group = heads * HD
    for k in range(parts):
        span = slice(k * width, (k + 1) * width)
        for h in range(heads):
            keys[h, span, :] = qkv[k, heads + h].astype(F32).T.astype(BF16)
            keys_t[h, :, span] = qkv[k, heads + h]
            vals_t[h, :, span] = qkv[k, 2 * heads + h]
    acc[group:, :] = jnp.zeros_like(acc[group:, :])
    count, listed = cols.shape
    per = count // parts
    for part in range(parts):

        for step in range(per):
            b = part * per + step
            at = slice(step * 128, (step + 1) * 128)
            into = slice(b * 128, (b + 1) * 128)
            spots = [
                pl.ds(pl.multiple_of(cols[b, n] * 128, 128), 128) for n in range(listed)
            ]
            for h in range(heads):
                d_t = d_att[part][h, :, at]
                query_t = qkv[part, h, :, at]
                val_t = jnp.concatenate([vals_t[h, :, s] for s in spots], axis=1)
                key = jnp.concatenate([keys[h, s, :] for s in spots], axis=0)
                d_probs = jnp.dot(
                    d_t.astype(F32).T.astype(BF16), val_t, preferred_element_type=F32
                )
                probs_low = probs_in[h, b]
                probs = probs_low.astype(F32)
                weighted = probs * d_probs
                delta = jnp.sum(weighted, axis=1, keepdims=True)
                d_scores = ((weighted - probs * delta) * SCALE).astype(BF16)
                d_query = jnp.dot(d_scores, key, preferred_element_type=F32)
                acc[h * HD : (h + 1) * HD, into] = d_query.T
                d_key = jnp.dot(query_t, d_scores, preferred_element_type=F32)
                d_val = jnp.dot(d_t, probs_low, preferred_element_type=F32)
                for n in range(listed):
                    block = slice(n * 128, (n + 1) * 128)
                    acc[(heads + h) * HD : (heads + h + 1) * HD, spots[n]] += d_key[:, block]
                    acc[(2 * heads + h) * HD : (2 * heads + h + 1) * HD, spots[n]] += d_val[:, block]

    left = acc[...].astype(BF16)
    for k in range(parts):
        out[k][...] = left[:, k * width : (k + 1) * width]
    total = rows[0].shape[1]
    for start in range(0, total, 256):
        span = slice(start, min(start + 256, total))
        right = jnp.concatenate([row[:, span] for row in rows], axis=0)
        store_rows(whole, start, jnp.dot(left, right, preferred_element_type=F32).T)
    emit_halves(index, whole, order, sent, kept)


def traded(pieces):
    count = len(pieces)
    return [pieces[0]] + [shifted(pieces[count - j], count - j) for j in range(1, count)]


def body(tokens, weights, cotangent, col_list, cut_lengths, keep_mask):
    parts, replicas = lax.axis_size("seq"), lax.axis_size("dp")
    z = lax.axis_index("seq")
    place = z.astype(jnp.int32).reshape(1)
    index = lax.axis_index("dp").astype(jnp.int32).reshape(1)
    inputs, upstream = tokens[0], cotangent[0]
    width, model = inputs.shape
    shard, _, wide = weights.shape
    group = wide // parts
    heads = group // HD
    orders = bit_orders(replicas)
    length = parts * width

    columns = col_list[0]
    count, listed = columns.shape
    turn = z * (count // parts)
    columns = jnp.roll((columns - turn) % count, -turn, axis=0)
    ends = jnp.cumsum(cut_lengths[0])
    spots = (jnp.arange(count, dtype=jnp.int32) + turn) % count
    owner = jnp.sum((ends[None, :] <= spots[:, None]).astype(jnp.int32), axis=1)
    same = (owner[columns] == owner[:, None]).astype(jnp.int32)
    bias = jnp.where(jnp.roll(keep_mask[0].reshape(count, 1, -1), -turn, axis=0) == 1, 0.0, LOW)

    low, high = call(
        functools.partial(shard_kernel, parts), (shape_of(shard, 2 * wide),) * 2, [],
        "ordered_shard", [place], [weights],
    )

    far = far_indices(orders)
    single = [r for r in far if bin(r).count("1") == 1]
    several = [r for r in far if bin(r).count("1") > 1]
    pieces = hop([inputs])
    lows = {r: [exchanged(low, r)] for r in single}
    lows[0] = [low]
    parted = [parted_for(lows, r, orders) for r in several]
    mark = call(mark_kernel, shape_of(8, 128), [], "mark", [], [pieces[1][:8, :128]], flops=1 << 36)
    pieces, lows, parted, mark = together(pieces, lows, parted, mark)

    while len(pieces) < parts - 1:
        pieces = hop(pieces)
    passed_on(lows, several, parted, orders)
    lows, high = together(lows, high)
    highs = {r: [exchanged(high, r)] for r in single}
    for r in far:
        lows[r | 1] = [exchanged(piece, 1) for piece in lows[r]]
    mark = call(mark_kernel, shape_of(8, 128), [], "mark", [], [pieces[-1][:8, :128]], flops=1 << 36)
    pieces, lows, mark = together(pieces, lows, mark)

    pieces = hop(pieces)
    low = in_order(lows, index)
    highs[0] = [high]
    passed_on(highs, several, [parted_for(highs, r, orders) for r in several], orders)
    for r in [0] + single:
        highs[r | 1] = [exchanged(highs[r][0], 1)]
    early = call(
        functools.partial(early_kernel, parts), shape_of(parts - 1, 3 * heads, HD, width),
        [], "early", [], [low] + pieces[:-1],
    )
    d_att = call(
        functools.partial(project_kernel, parts, group),
        (shape_of(group, width),) * parts, [], "project", [], [upstream, low],
    )
    pieces, d_att, early, highs = together(pieces, d_att, early, highs)

    d_att = [d.reshape(heads, HD, width) for d in traded(d_att)]
    results = call(
        functools.partial(forward_kernel, parts, heads),
        (shape_of(parts, 3 * heads, HD, width),)
        + (shape_of(heads, HD, width),) * parts
        + (shape_of(heads, count, 128, listed * 128),),
        [pltpu.VMEM((heads, HD, length), BF16), pltpu.VMEM((heads, length, HD), BF16)],
        "attend", [columns, same], [bias, low, pieces[-1], early],
        flops=1 << 34,
    )
    d_att, results, highs = together(d_att, results, highs)
    qkv, att, probs = results[0], results[1:-1], results[-1]

    att = traded([a.reshape(group, width) for a in att])
    halved = (replicas // 2, shard, 3 * group)
    back = call(
        functools.partial(backward_kernel, parts, heads, orders[0]),
        (shape_of(3 * group, width),) * parts + (shape_of(*halved), shape_of(*halved, dtype=F32)),
        [
            pltpu.VMEM((heads, length, HD), BF16),
            pltpu.VMEM((heads, HD, length), BF16),
            pltpu.VMEM((heads, HD, length), BF16),
            pltpu.VMEM((3 * group, length), F32),
            pltpu.VMEM((replicas, shard, 3 * group), F32),
        ],
        "attend_back", [columns, index], [qkv, probs] + pieces + list(d_att), flops=1 << 34, limit=24,
    )
    att, back, highs = together(att, back, highs)
    for r in several:
        highs[r | 1] = [exchanged(piece, 1) for piece in highs[r]]

    d_qkv, sent, inner_sum = back[:parts], back[parts], back[parts + 1]
    d_here = [d_qkv[0]] + [None] * (parts - 1)
    def fetch(which):
        for j in which:
            d_here[j] = shifted(d_qkv[parts - j], parts - j)

    fetch([1, parts - 1])
    inner_more = exchanged(sent, 1)
    sent, outer_sum = gradient_halves(
        functools.partial(outer_gradient_kernel, parts, orders[0]), "outer_gradient", wide,
        [index], [upstream] + list(att), replicas,
    )
    outer_more = exchanged(sent, 1)
    cut = 3 * group
    away = block_order(orders[0])[:-1]
    kept, *given = call(
        functools.partial(combine_kernel, cut),
        (shape_of(shard, cut + wide, dtype=F32),) + (shape_of(shard, cut + wide),) * len(away),
        [], "combine", [], [inner_sum, inner_more, outer_sum, outer_more], flops=1 << 33,
    )
    arrived = [exchanged(piece, r) for piece, r in zip(given, away)]
    d_qkv, d_here[1] = together(d_qkv, d_here[1])
    fetch(range(2, parts - 1))
    inner_own, *pieces = call(
        functools.partial(finish_kernel, cut, group),
        (shape_of(shard, cut),) + (shape_of(shard, group),) * parts,
        [], "finish", [], [kept] + arrived,
    )
    pieces, d_here = together(pieces, d_here)

    own = call(own_kernel, shape_of(shard, cut + group), [], "own", [], [inner_own] + traded(pieces))
    own, att = together(own, att)
    found = [own] + [shifted(own, parts - j) for j in range(1, parts)]
    result = call(
        functools.partial(result_kernel, parts, group),
        shape_of(width, model), [pltpu.VMEM((wide, width), F32)], "result", [],
        [low] + list(att), flops=1 << 32,
    )
    high = in_order(highs, index)
    grad_in = call(
        functools.partial(grad_in_kernel, parts, group),
        shape_of(width, model), [pltpu.VMEM((3 * wide, width), F32)],
        "grad_in", [], [low, high] + list(d_here), flops=1 << 33, limit=20,
    )
    grad_all = call(
        functools.partial(final_kernel, parts, replicas),
        shape_of(shard, 4, wide, dtype=F32), [], "final_rows", [place], found,
    )
    return (result[None], grad_in[None], grad_all)


def solution(mesh):
    placed = (
        P("dp", "seq", None),
        P("dp", None, None),
        P("dp", "seq", None),
        P("dp", None, None),
        P("dp", None),
        P("dp", None),
    )
    return jax.shard_map(
        body,
        mesh=mesh,
        in_specs=placed,
        out_specs=(P("dp", "seq", None), P("dp", "seq", None), P("dp", None, None)),
        check_vma=False,
    )
```

```python
import functools
import math

import jax
import jax.numpy as jnp
from jax import lax
from jax.experimental import pallas as pl
from jax.experimental.pallas import tpu as pltpu
from jax.sharding import PartitionSpec as P

HD = 88
SCALE = 1.0 / math.sqrt(HD)
LOG2E = math.log2(math.e)
LOW = -1e30
F32 = jnp.float32
BF16 = jnp.bfloat16


def shifted(array, step):
    count = lax.axis_size("seq")
    return lax.ppermute(array, "seq", [(i, (i + step) % count) for i in range(count)])


def exchanged(array, bit):
    count = lax.axis_size("dp")
    return lax.ppermute(array, "dp", [(i, i ^ bit) for i in range(count)])


def bit_orders(count):
    far = [1 << i for i in range(1, count.bit_length() - 1)]
    half = len(far) // 2
    return far, far[half:] + far[:half]


def block_order(bits):
    if not bits:
        return [0]
    rest = block_order(bits[1:])
    return [r | bits[0] for r in rest] + rest


VMEM = pl.BlockSpec(memory_space=pltpu.VMEM)
SMEM = pl.BlockSpec(memory_space=pltpu.SMEM)


def call(kernel, out_shape, scratch, name, scalars, arrays, flops=1, limit=16):
    single = not isinstance(out_shape, tuple)
    return pl.pallas_call(
        kernel,
        out_shape=out_shape,
        in_specs=[SMEM] * len(scalars) + [VMEM] * len(arrays),
        out_specs=VMEM if single else (VMEM,) * len(out_shape),
        scratch_shapes=scratch,
        compiler_params=pltpu.CompilerParams(vmem_limit_bytes=limit << 20),
        cost_estimate=pl.CostEstimate(flops=flops, bytes_accessed=1, transcendentals=0),
        name=name,
    )(*scalars, *arrays)


def together(*trees):
    return lax.optimization_barrier(trees)


def shape_of(*dims, dtype=BF16):
    return jax.ShapeDtypeStruct(dims, dtype)


def far_indices(orders):
    return sorted(range(0, 2 << len(orders[0]), 2), key=lambda r: (bin(r).count("1"), r))


def parting_kernel(spans, *refs):
    count = len(spans)
    for span, piece, out in zip(spans, refs[:count], refs[count:]):
        out[...] = piece[:, span]


def parted_for(held, r, orders):
    half = held[0][0].shape[1] // 2
    parts = []
    for n, order in enumerate(orders):
        source = held.get(r ^ max((b for b in order if b & r), key=order.index))
        if source is None:
            return None
        whole = len(source) == 1
        parts.append((source[0], slice(n * half, (n + 1) * half)) if whole else (source[n], slice(None)))
    return call(
        functools.partial(parting_kernel, [span for _, span in parts]),
        (shape_of(parts[0][0].shape[0], half),) * 2, [], "parting", [],
        [piece for piece, _ in parts],
    )


def passed_on(held, several, parted, orders):
    for r, halves in zip(several, parted):
        halves = halves or parted_for(held, r, orders)
        last = [max((b for b in order if b & r), key=order.index) for order in orders]
        held[r] = [exchanged(halves[n], last[n]) for n in range(2)]


def in_order_kernel(sizes, index, *refs):
    pieces, out, at = refs[:-1], refs[-1], 0
    half = out.shape[2] // 2
    for r, size in sizes:
        if size == 1:
            out[index[0] ^ r] = pieces[at][...]
        else:
            out[index[0] ^ r, :, :half] = pieces[at][...]
            out[index[0] ^ r, :, half:] = pieces[at + 1][...]
        at += size


def in_order(held, index, flops=1):
    count, (rows, columns) = len(held), held[0][0].shape
    out = call(
        functools.partial(in_order_kernel, [(r, len(held[r])) for r in held]),
        shape_of(count, rows, columns), [], "in_order", [index],
        [piece for r in held for piece in held[r]], flops=flops,
    )
    return out.reshape(count * rows, columns)


def mark_kernel(piece, out):
    out[...] = piece[...]


def shard_kernel(parts, place, weights, low, high):
    group = weights.shape[2] // parts
    for z in range(parts):

        @pl.when(place[0] == z)
        def _():
            cols = [weights[:, c, :] for c in range(4)]

            def block(c, j):
                start = (z + j) % parts * group
                return cols[c][:, start : start + group]

            chosen = [block(c, 0) for c in range(3)] + [block(3, j) for j in range(parts)]
            chosen += [block(c, j) for j in range(1, parts) for c in range(3)]
            low[...] = jnp.concatenate(chosen[: 2 * parts], axis=1)
            high[...] = jnp.concatenate(chosen[2 * parts :], axis=1)


def project_kernel(parts, group, rows, low, *out):
    outer = low[:, 3 * group : (3 + parts) * group]
    total = jnp.dot(rows[...], outer, preferred_element_type=F32).T
    for j in range(parts):
        out[j][...] = total[j * group : (j + 1) * group].astype(BF16)


def result_kernel(parts, group, low, *refs):
    att, (out, scratch) = refs[:parts], refs[parts:]
    for j in range(parts):
        scratch[j * group : (j + 1) * group, :] = att[j][...].astype(F32)
    left = scratch[...].T.astype(BF16)
    outer = low[:, 3 * group : (3 + parts) * group]
    out[...] = lax.dot_general(
        left, outer, (((1,), (1,)), ((), ())), preferred_element_type=F32
    ).astype(BF16)


def grad_in_kernel(parts, group, low, high, *refs):
    d_here, (out, scratch) = refs[:parts], refs[parts:]
    for j in range(parts):
        scratch[j * 3 * group : (j + 1) * 3 * group, :] = d_here[j][...].astype(F32)
    left = scratch[...].T.astype(BF16)
    first, rest = 3 * group, left.shape[1] - high.shape[1]
    contract = (((1,), (1,)), ((), ()))
    total = lax.dot_general(
        left[:, rest:], high[...], contract, preferred_element_type=F32
    )
    total += lax.dot_general(
        left[:, :first], low[:, :first], contract, preferred_element_type=F32
    )
    if rest > first:
        total += lax.dot_general(
            left[:, first:rest], low[:, (3 + parts) * group :], contract,
            preferred_element_type=F32,
        )
    out[...] = total.astype(BF16)


def store_rows(whole, start, value):
    rows, end = whole.shape[1], start + value.shape[0]
    at = start
    while at < end:
        block, first = divmod(at, rows)
        size = min(rows - first, end - at)
        whole[block, first : first + size, :] = value[at - start : at - start + size]
        at += size


def emit_halves(index, whole, order, sent, kept):
    for i, r in enumerate(block_order(order)):
        mine = index[0] ^ r
        kept[i] = whole[mine]
        sent[i] = whole[mine ^ 1].astype(BF16)


def outer_gradient_kernel(parts, order, index, rows, *refs):
    att, (sent, kept, whole) = refs[:parts], refs[parts:]
    left = jnp.concatenate([a[...] for a in att], axis=0)
    for start in range(0, rows.shape[1], 256):
        span = slice(start, min(start + 256, rows.shape[1]))
        store_rows(whole, start, jnp.dot(left, rows[:, span], preferred_element_type=F32).T)
    emit_halves(index, whole, order, sent, kept)


def gradient_halves(kernel, name, columns, scalars, arrays, replicas):
    width = arrays[0].shape[-1]
    shape = (replicas // 2, width // replicas, columns)
    return call(
        kernel, (shape_of(*shape), shape_of(*shape, dtype=F32)),
        [pltpu.VMEM((replicas, width // replicas, columns), F32)], name, scalars, arrays, flops=1 << 34,
    )


def combine_kernel(cut, inner, inner_more, outer, outer_more, kept, *out):
    count = inner.shape[0]
    for i in range(count):
        left = inner[i] + inner_more[i].astype(F32)
        right = outer[i] + outer_more[i].astype(F32)
        if i < count - 1:
            out[i][:, :cut] = left.astype(BF16)
            out[i][:, cut:] = right.astype(BF16)
        else:
            kept[:, :cut] = left
            kept[:, cut:] = right


def finish_kernel(cut, group, kept, *refs):
    parts = (kept.shape[1] - cut) // group
    arrived, (inner, *outer) = refs[: -parts - 1], refs[-parts - 1 :]
    total = kept[...]
    for more in arrived:
        total += more[...].astype(F32)
    half = total.shape[0] // 2
    inner[...] = total[:, :cut].astype(BF16)
    for j in range(parts):
        span = slice(cut + j * group, cut + (j + 1) * group)
        outer[j][...] = jnp.concatenate([total[:half, span], total[half:, span]], axis=1).astype(BF16)


def own_kernel(inner, *refs):
    pieces, out = refs[:-1], refs[-1]
    half, group = pieces[0].shape[0], pieces[0].shape[1] // 2
    total = pieces[0][...].astype(F32)
    for piece in pieces[1:]:
        total += piece[...].astype(F32)
    first = inner[...].astype(F32)
    out[...] = jnp.concatenate(
        [first[:half], total[:, :group], first[half:], total[:, group:]], axis=1
    ).astype(BF16)


def final_kernel(parts, replicas, place, *refs):
    found, out = refs[:-1], refs[-1]
    group = out.shape[2] // parts
    for z in range(parts):

        @pl.when(place[0] == z)
        def _():
            turn = [(hg - z) % parts for hg in range(parts)]
            half, wide = found[0].shape[0], found[0].shape[1] // 2
            for c in range(4):
                for n in range(2):
                    span = slice(n * wide + c * group, n * wide + (c + 1) * group)
                    out[n * half : (n + 1) * half, c, :] = jnp.concatenate(
                        [found[j][:, span].astype(F32) for j in turn], axis=1
                    ) * (1.0 / replicas)


def hop(pieces):
    return pieces + [shifted(pieces[-1], -1)]


def store_projection(qkv, k, rows, own):
    total = jnp.dot(rows[...], own, preferred_element_type=F32).T
    for i in range(qkv.shape[1]):
        qkv[k, i] = total[i * HD : (i + 1) * HD].astype(BF16)


def early_kernel(parts, low, *refs):
    pieces, qkv = refs[: parts - 1], refs[-1]
    own = low[:, : qkv.shape[1] * HD]
    for k in range(parts - 1):
        store_projection(qkv, k, pieces[k], own)


def forward_kernel(parts, heads, cols, same, bias, low, piece, early, *refs):
    qkv, att_out = refs[0], refs[1 : parts + 1]
    probs_out, keys, vals = refs[parts + 1 :]
    group, width = heads * HD, qkv.shape[3]
    for k in range(parts - 1):
        qkv[k] = early[k]
    store_projection(qkv, parts - 1, piece, low[:, : 3 * group])
    for k in range(parts):
        span = slice(k * width, (k + 1) * width)
        for h in range(heads):
            keys[h, :, span] = qkv[k, heads + h]
            vals[h, span, :] = qkv[k, 2 * heads + h].astype(F32).T.astype(BF16)
    count, listed = cols.shape
    per = count // parts
    line = lax.broadcasted_iota(jnp.int32, (128, 128), 0)
    lanes = lax.broadcasted_iota(jnp.int32, (128, 128), 1)
    diagonal = line == lanes
    for part in range(parts):

        for step in range(per):
            b = part * per + step
            at = slice(step * 128, (step + 1) * 128)
            spots = [cols[b, n] for n in range(listed)]
            pens = [
                bias[spots[n]] + jnp.where(same[b, n] == 1, 0.0, LOW) for n in range(listed)
            ]
            first = jnp.where(diagonal, 0.0, jnp.broadcast_to(pens[0], (128, 128)))
            for h in range(heads):
                query = qkv[part, h, :, at].astype(F32).T.astype(BF16)
                key_t = jnp.concatenate(
                    [keys[h, :, pl.ds(pl.multiple_of(s * 128, 128), 128)] for s in spots], axis=1
                )
                val = jnp.concatenate(
                    [vals[h, pl.ds(pl.multiple_of(s * 128, 128), 128), :] for s in spots], axis=0
                )
                scores = jnp.dot(query, key_t, preferred_element_type=F32) * (SCALE * LOG2E)
                scores = jnp.concatenate(
                    [scores[:, :128] + first]
                    + [scores[:, n * 128 : (n + 1) * 128] + pens[n] for n in range(1, listed)],
                    axis=1,
                )
                largest = jnp.max(scores, axis=1, keepdims=True)
                expd = jnp.exp2(scores - largest)
                probs = expd * (1.0 / jnp.sum(expd, axis=1, keepdims=True))
                probs = probs.astype(BF16)
                probs_out[h, b] = probs
                att = jnp.dot(probs, val, preferred_element_type=F32)
                att_out[part][h, :, at] = att.T.astype(BF16)


def backward_kernel(parts, heads, order, cols, index, qkv, probs_in, *refs):
    rows, d_att, out = refs[:parts], refs[parts : 2 * parts], refs[2 * parts : 3 * parts]
    sent, kept, keys, keys_t, vals_t, acc, whole = refs[3 * parts :]
    width = qkv.shape[3]
    group = heads * HD
    for k in range(parts):
        span = slice(k * width, (k + 1) * width)
        for h in range(heads):
            keys[h, span, :] = qkv[k, heads + h].astype(F32).T.astype(BF16)
            keys_t[h, :, span] = qkv[k, heads + h]
            vals_t[h, :, span] = qkv[k, 2 * heads + h]
    acc[group:, :] = jnp.zeros_like(acc[group:, :])
    count, listed = cols.shape
    per = count // parts
    for part in range(parts):

        for step in range(per):
            b = part * per + step
            at = slice(step * 128, (step + 1) * 128)
            into = slice(b * 128, (b + 1) * 128)
            spots = [
                pl.ds(pl.multiple_of(cols[b, n] * 128, 128), 128) for n in range(listed)
            ]
            for h in range(heads):
                d_t = d_att[part][h, :, at]
                query_t = qkv[part, h, :, at]
                val_t = jnp.concatenate([vals_t[h, :, s] for s in spots], axis=1)
                key = jnp.concatenate([keys[h, s, :] for s in spots], axis=0)
                d_probs = jnp.dot(
                    d_t.astype(F32).T.astype(BF16), val_t, preferred_element_type=F32
                )
                probs_low = probs_in[h, b]
                probs = probs_low.astype(F32)
                weighted = probs * d_probs
                delta = jnp.sum(weighted, axis=1, keepdims=True)
                d_scores = (probs * (d_probs - delta)).astype(BF16)
                d_query = jnp.dot(d_scores, key, preferred_element_type=F32)
                acc[h * HD : (h + 1) * HD, into] = d_query.T * SCALE
                d_key = jnp.dot(query_t, d_scores, preferred_element_type=F32)
                d_val = jnp.dot(d_t, probs_low, preferred_element_type=F32)
                for n in range(listed):
                    block = slice(n * 128, (n + 1) * 128)
                    acc[(heads + h) * HD : (heads + h + 1) * HD, spots[n]] += d_key[:, block]
                    acc[(2 * heads + h) * HD : (2 * heads + h + 1) * HD, spots[n]] += d_val[:, block]

    acc[group : 2 * group, :] = acc[group : 2 * group, :] * SCALE
    left = acc[...].astype(BF16)
    for k in range(parts):
        out[k][...] = left[:, k * width : (k + 1) * width]
    total = rows[0].shape[1]
    for start in range(0, total, 256):
        span = slice(start, min(start + 256, total))
        right = jnp.concatenate([row[:, span] for row in rows], axis=0)
        store_rows(whole, start, jnp.dot(left, right, preferred_element_type=F32).T)
    emit_halves(index, whole, order, sent, kept)


def traded(pieces):
    count = len(pieces)
    return [pieces[0]] + [shifted(pieces[count - j], count - j) for j in range(1, count)]


def body(tokens, weights, cotangent, col_list, cut_lengths, keep_mask):
    parts, replicas = lax.axis_size("seq"), lax.axis_size("dp")
    z = lax.axis_index("seq")
    place = z.astype(jnp.int32).reshape(1)
    index = lax.axis_index("dp").astype(jnp.int32).reshape(1)
    inputs, upstream = tokens[0], cotangent[0]
    width, model = inputs.shape
    shard, _, wide = weights.shape
    group = wide // parts
    heads = group // HD
    orders = bit_orders(replicas)
    length = parts * width

    columns = col_list[0]
    count, listed = columns.shape
    turn = z * (count // parts)
    columns = jnp.roll((columns - turn) % count, -turn, axis=0)
    ends = jnp.cumsum(cut_lengths[0])
    spots = (jnp.arange(count, dtype=jnp.int32) + turn) % count
    owner = jnp.sum((ends[None, :] <= spots[:, None]).astype(jnp.int32), axis=1)
    same = (owner[columns] == owner[:, None]).astype(jnp.int32)
    bias = jnp.where(jnp.roll(keep_mask[0].reshape(count, 1, -1), -turn, axis=0) == 1, 0.0, LOW)

    low, high = call(
        functools.partial(shard_kernel, parts), (shape_of(shard, 2 * wide),) * 2, [],
        "ordered_shard", [place], [weights],
    )

    far = far_indices(orders)
    single = [r for r in far if bin(r).count("1") == 1]
    several = [r for r in far if bin(r).count("1") > 1]
    pieces = hop([inputs])
    lows = {r: [exchanged(low, r)] for r in single}
    lows[0] = [low]
    parted = [parted_for(lows, r, orders) for r in several]
    mark = call(mark_kernel, shape_of(8, 128), [], "mark", [], [pieces[1][:8, :128]], flops=1 << 34)
    pieces, lows, parted, mark = together(pieces, lows, parted, mark)

    while len(pieces) < parts - 1:
        pieces = hop(pieces)
    passed_on(lows, several, parted, orders)
    lows, high = together(lows, high)
    highs = {r: [exchanged(high, r)] for r in single}
    for r in far:
        lows[r | 1] = [exchanged(piece, 1) for piece in lows[r]]
    mark = call(mark_kernel, shape_of(8, 128), [], "mark", [], [pieces[-1][:8, :128]], flops=1 << 34)
    pieces, lows, mark = together(pieces, lows, mark)

    pieces = hop(pieces)
    low = in_order(lows, index)
    highs[0] = [high]
    passed_on(highs, several, [parted_for(highs, r, orders) for r in several], orders)
    for r in [0] + single:
        highs[r | 1] = [exchanged(highs[r][0], 1)]
    early = call(
        functools.partial(early_kernel, parts), shape_of(parts - 1, 3 * heads, HD, width),
        [], "early", [], [low] + pieces[:-1],
    )
    d_att = call(
        functools.partial(project_kernel, parts, group),
        (shape_of(group, width),) * parts, [], "project", [], [upstream, low],
    )
    pieces, d_att, early, highs = together(pieces, d_att, early, highs)

    d_att = [d.reshape(heads, HD, width) for d in traded(d_att)]
    results = call(
        functools.partial(forward_kernel, parts, heads),
        (shape_of(parts, 3 * heads, HD, width),)
        + (shape_of(heads, HD, width),) * parts
        + (shape_of(heads, count, 128, listed * 128),),
        [pltpu.VMEM((heads, HD, length), BF16), pltpu.VMEM((heads, length, HD), BF16)],
        "attend", [columns, same], [bias, low, pieces[-1], early],
        flops=1 << 34,
    )
    d_att, results, highs = together(d_att, results, highs)
    qkv, att, probs = results[0], results[1:-1], results[-1]

    att = traded([a.reshape(group, width) for a in att])
    halved = (replicas // 2, shard, 3 * group)
    back = call(
        functools.partial(backward_kernel, parts, heads, orders[0]),
        (shape_of(3 * group, width),) * parts + (shape_of(*halved), shape_of(*halved, dtype=F32)),
        [
            pltpu.VMEM((heads, length, HD), BF16),
            pltpu.VMEM((heads, HD, length), BF16),
            pltpu.VMEM((heads, HD, length), BF16),
            pltpu.VMEM((3 * group, length), F32),
            pltpu.VMEM((replicas, shard, 3 * group), F32),
        ],
        "attend_back", [columns, index], [qkv, probs] + pieces + list(d_att), flops=1 << 34, limit=24,
    )
    att, back, highs = together(att, back, highs)
    for r in several:
        highs[r | 1] = [exchanged(piece, 1) for piece in highs[r]]

    d_qkv, sent, inner_sum = back[:parts], back[parts], back[parts + 1]
    d_here = [d_qkv[0]] + [None] * (parts - 1)
    def fetch(which):
        for j in which:
            d_here[j] = shifted(d_qkv[parts - j], parts - j)

    fetch([1, parts - 1])
    inner_more = exchanged(sent, 1)
    sent, outer_sum = gradient_halves(
        functools.partial(outer_gradient_kernel, parts, orders[0]), "outer_gradient", wide,
        [index], [upstream] + list(att), replicas,
    )
    outer_more = exchanged(sent, 1)
    cut = 3 * group
    away = block_order(orders[0])[:-1]
    kept, *given = call(
        functools.partial(combine_kernel, cut),
        (shape_of(shard, cut + wide, dtype=F32),) + (shape_of(shard, cut + wide),) * len(away),
        [], "combine", [], [inner_sum, inner_more, outer_sum, outer_more], flops=1 << 33,
    )
    arrived = [exchanged(piece, r) for piece, r in zip(given, away)]
    d_qkv, d_here[1] = together(d_qkv, d_here[1])
    fetch(range(2, parts - 1))
    inner_own, *pieces = call(
        functools.partial(finish_kernel, cut, group),
        (shape_of(shard, cut),) + (shape_of(shard // 2, 2 * group),) * parts,
        [], "finish", [], [kept] + arrived,
    )
    pieces, d_here = together(pieces, d_here)

    own = call(
        own_kernel, shape_of(shard // 2, 2 * (cut + group)), [], "own", [], [inner_own] + traded(pieces)
    )
    own, att = together(own, att)
    found = [own] + [shifted(own, parts - j) for j in range(1, parts)]
    result = call(
        functools.partial(result_kernel, parts, group),
        shape_of(width, model), [pltpu.VMEM((wide, width), F32)], "result", [],
        [low] + list(att), flops=1 << 32,
    )
    high = in_order(highs, index)
    grad_in = call(
        functools.partial(grad_in_kernel, parts, group),
        shape_of(width, model), [pltpu.VMEM((3 * wide, width), F32)],
        "grad_in", [], [low, high] + list(d_here), flops=1 << 33, limit=20,
    )
    grad_all = call(
        functools.partial(final_kernel, parts, replicas),
        shape_of(shard, 4, wide, dtype=F32), [], "final_rows", [place], found,
    )
    return (result[None], grad_in[None], grad_all)


def solution(mesh):
    placed = (
        P("dp", "seq", None),
        P("dp", None, None),
        P("dp", "seq", None),
        P("dp", None, None),
        P("dp", None),
        P("dp", None),
    )
    return jax.shard_map(
        body,
        mesh=mesh,
        in_specs=placed,
        out_specs=(P("dp", "seq", None), P("dp", "seq", None), P("dp", None, None)),
        check_vma=False,
    )
```

```python
import functools
import math

import jax
import jax.numpy as jnp
from jax import lax
from jax.experimental import pallas as pl
from jax.experimental.pallas import tpu as pltpu
from jax.sharding import PartitionSpec as P

HD = 88
SCALE = 1.0 / math.sqrt(HD)
LOG2E = math.log2(math.e)
LOW = -1e30
F32 = jnp.float32
BF16 = jnp.bfloat16


def shifted(array, step):
    count = lax.axis_size("seq")
    return lax.ppermute(array, "seq", [(i, (i + step) % count) for i in range(count)])


def exchanged(array, bit):
    count = lax.axis_size("dp")
    return lax.ppermute(array, "dp", [(i, i ^ bit) for i in range(count)])


def bit_orders(count):
    far = [1 << i for i in range(1, count.bit_length() - 1)]
    half = len(far) // 2
    return far, far[half:] + far[:half]


def block_order(bits):
    if not bits:
        return [0]
    rest = block_order(bits[1:])
    return [r | bits[0] for r in rest] + rest


VMEM = pl.BlockSpec(memory_space=pltpu.VMEM)
SMEM = pl.BlockSpec(memory_space=pltpu.SMEM)


def call(kernel, out_shape, scratch, name, scalars, arrays, flops=1, limit=16):
    single = not isinstance(out_shape, tuple)
    return pl.pallas_call(
        kernel,
        out_shape=out_shape,
        in_specs=[SMEM] * len(scalars) + [VMEM] * len(arrays),
        out_specs=VMEM if single else (VMEM,) * len(out_shape),
        scratch_shapes=scratch,
        compiler_params=pltpu.CompilerParams(vmem_limit_bytes=limit << 20),
        cost_estimate=pl.CostEstimate(flops=flops, bytes_accessed=1, transcendentals=0),
        name=name,
    )(*scalars, *arrays)


def together(*trees):
    return lax.optimization_barrier(trees)


def shape_of(*dims, dtype=BF16):
    return jax.ShapeDtypeStruct(dims, dtype)


def far_indices(orders):
    return sorted(range(0, 2 << len(orders[0]), 2), key=lambda r: (bin(r).count("1"), r))


def parting_kernel(spans, *refs):
    count = len(spans)
    for span, piece, out in zip(spans, refs[:count], refs[count:]):
        out[...] = piece[:, span]


def parted_for(held, r, orders):
    half = held[0][0].shape[1] // 2
    parts = []
    for n, order in enumerate(orders):
        source = held.get(r ^ max((b for b in order if b & r), key=order.index))
        if source is None:
            return None
        whole = len(source) == 1
        parts.append((source[0], slice(n * half, (n + 1) * half)) if whole else (source[n], slice(None)))
    return call(
        functools.partial(parting_kernel, [span for _, span in parts]),
        (shape_of(parts[0][0].shape[0], half),) * 2, [], "parting", [],
        [piece for piece, _ in parts],
    )


def passed_on(held, several, parted, orders):
    for r, halves in zip(several, parted):
        halves = halves or parted_for(held, r, orders)
        last = [max((b for b in order if b & r), key=order.index) for order in orders]
        held[r] = [exchanged(halves[n], last[n]) for n in range(2)]


def in_order_kernel(sizes, index, *refs):
    pieces, out, at = refs[:-1], refs[-1], 0
    half = out.shape[2] // 2
    for r, size in sizes:
        if size == 1:
            out[index[0] ^ r] = pieces[at][...]
        else:
            out[index[0] ^ r, :, :half] = pieces[at][...]
            out[index[0] ^ r, :, half:] = pieces[at + 1][...]
        at += size


def in_order(held, index, flops=1):
    count, (rows, columns) = len(held), held[0][0].shape
    out = call(
        functools.partial(in_order_kernel, [(r, len(held[r])) for r in held]),
        shape_of(count, rows, columns), [], "in_order", [index],
        [piece for r in held for piece in held[r]], flops=flops,
    )
    return out.reshape(count * rows, columns)


def mark_kernel(piece, out):
    out[...] = piece[...]


def shard_kernel(parts, place, weights, low, high):
    group = weights.shape[2] // parts
    for z in range(parts):

        @pl.when(place[0] == z)
        def _():
            cols = [weights[:, c, :] for c in range(4)]

            def block(c, j):
                start = (z + j) % parts * group
                return cols[c][:, start : start + group]

            chosen = [block(c, 0) for c in range(3)] + [block(3, j) for j in range(parts)]
            chosen += [block(c, j) for j in range(1, parts) for c in range(3)]
            low[...] = jnp.concatenate(chosen[: 2 * parts], axis=1)
            high[...] = jnp.concatenate(chosen[2 * parts :], axis=1)


def project_kernel(parts, group, rows, low, *out):
    outer = low[:, 3 * group : (3 + parts) * group]
    total = jnp.dot(rows[...], outer, preferred_element_type=F32).T
    for j in range(parts):
        out[j][...] = total[j * group : (j + 1) * group].astype(BF16)


def result_kernel(parts, group, low, *refs):
    att, (out, scratch) = refs[:parts], refs[parts:]
    for j in range(parts):
        scratch[j * group : (j + 1) * group, :] = att[j][...].astype(F32)
    left = scratch[...].T.astype(BF16)
    outer = low[:, 3 * group : (3 + parts) * group]
    out[...] = lax.dot_general(
        left, outer, (((1,), (1,)), ((), ())), preferred_element_type=F32
    ).astype(BF16)


def grad_in_kernel(parts, group, low, high, *refs):
    d_here, (out, scratch) = refs[:parts], refs[parts:]
    for j in range(parts):
        scratch[j * 3 * group : (j + 1) * 3 * group, :] = d_here[j][...].astype(F32)
    left = scratch[...].T.astype(BF16)
    first, rest = 3 * group, left.shape[1] - high.shape[1]
    contract = (((1,), (1,)), ((), ()))
    total = lax.dot_general(
        left[:, rest:], high[...], contract, preferred_element_type=F32
    )
    total += lax.dot_general(
        left[:, :first], low[:, :first], contract, preferred_element_type=F32
    )
    if rest > first:
        total += lax.dot_general(
            left[:, first:rest], low[:, (3 + parts) * group :], contract,
            preferred_element_type=F32,
        )
    out[...] = total.astype(BF16)


def store_rows(whole, start, value):
    rows, end = whole.shape[1], start + value.shape[0]
    at = start
    while at < end:
        block, first = divmod(at, rows)
        size = min(rows - first, end - at)
        whole[block, first : first + size, :] = value[at - start : at - start + size]
        at += size


def emit_halves(index, whole, order, sent, kept):
    for i, r in enumerate(block_order(order)):
        mine = index[0] ^ r
        kept[i] = whole[mine]
        sent[i] = whole[mine ^ 1].astype(BF16)


def outer_gradient_kernel(parts, order, index, rows, *refs):
    att, (sent, kept, whole) = refs[:parts], refs[parts:]
    left = jnp.concatenate([a[...] for a in att], axis=0)
    for start in range(0, rows.shape[1], 256):
        span = slice(start, min(start + 256, rows.shape[1]))
        store_rows(whole, start, jnp.dot(left, rows[:, span], preferred_element_type=F32).T)
    emit_halves(index, whole, order, sent, kept)


def gradient_halves(kernel, name, columns, scalars, arrays, replicas):
    width = arrays[0].shape[-1]
    shape = (replicas // 2, width // replicas, columns)
    return call(
        kernel, (shape_of(*shape), shape_of(*shape, dtype=F32)),
        [pltpu.VMEM((replicas, width // replicas, columns), F32)], name, scalars, arrays, flops=1 << 34,
    )


def combine_kernel(cut, inner, inner_more, outer, outer_more, kept, *out):
    count = inner.shape[0]
    for i in range(count):
        left = inner[i] + inner_more[i].astype(F32)
        right = outer[i] + outer_more[i].astype(F32)
        if i < count - 1:
            out[i][:, :cut] = left.astype(BF16)
            out[i][:, cut:] = right.astype(BF16)
        else:
            kept[:, :cut] = left
            kept[:, cut:] = right


def finish_kernel(cut, group, kept, *refs):
    parts = (kept.shape[1] - cut) // group
    arrived, (inner, *outer) = refs[: -parts - 1], refs[-parts - 1 :]
    total = kept[...]
    for more in arrived:
        total += more[...].astype(F32)
    half = total.shape[0] // 2
    inner[...] = total[:, :cut].astype(BF16)
    for j in range(parts):
        span = slice(cut + j * group, cut + (j + 1) * group)
        outer[j][...] = jnp.concatenate([total[:half, span], total[half:, span]], axis=1).astype(BF16)


def own_kernel(inner, *refs):
    pieces, out = refs[:-1], refs[-1]
    half, group = pieces[0].shape[0], pieces[0].shape[1] // 2
    total = pieces[0][...].astype(F32)
    for piece in pieces[1:]:
        total += piece[...].astype(F32)
    first = inner[...].astype(F32)
    out[...] = jnp.concatenate(
        [first[:half], total[:, :group], first[half:], total[:, group:]], axis=1
    ).astype(BF16)


def final_kernel(parts, replicas, place, *refs):
    found, out = refs[:-1], refs[-1]
    group = out.shape[2] // parts
    for z in range(parts):

        @pl.when(place[0] == z)
        def _():
            turn = [(hg - z) % parts for hg in range(parts)]
            half, wide = found[0].shape[0], found[0].shape[1] // 2
            for c in range(4):
                for n in range(2):
                    span = slice(n * wide + c * group, n * wide + (c + 1) * group)
                    out[n * half : (n + 1) * half, c, :] = jnp.concatenate(
                        [found[j][:, span].astype(F32) for j in turn], axis=1
                    ) * (1.0 / replicas)


def hop(pieces):
    return pieces + [shifted(pieces[-1], -1)]


def store_projection(qkv, k, rows, own):
    total = jnp.dot(rows[...], own, preferred_element_type=F32).T
    for i in range(qkv.shape[1]):
        qkv[k, i] = total[i * HD : (i + 1) * HD].astype(BF16)


def early_kernel(parts, low, *refs):
    pieces, qkv = refs[: parts - 1], refs[-1]
    own = low[:, : qkv.shape[1] * HD]
    for k in range(parts - 1):
        store_projection(qkv, k, pieces[k], own)


def forward_kernel(parts, heads, cols, same, bias, low, piece, early, *refs):
    qkv, att_out = refs[0], refs[1 : parts + 1]
    probs_out, keys, vals = refs[parts + 1 :]
    group, width = heads * HD, qkv.shape[3]
    for k in range(parts - 1):
        qkv[k] = early[k]
    store_projection(qkv, parts - 1, piece, low[:, : 3 * group])
    for k in range(parts):
        span = slice(k * width, (k + 1) * width)
        for h in range(heads):
            keys[h, :, span] = qkv[k, heads + h]
            vals[h, span, :] = qkv[k, 2 * heads + h].astype(F32).T.astype(BF16)
    count, listed = cols.shape
    per = count // parts
    line = lax.broadcasted_iota(jnp.int32, (128, 128), 0)
    lanes = lax.broadcasted_iota(jnp.int32, (128, 128), 1)
    diagonal = line == lanes
    for part in range(parts):

        for step in range(per):
            b = part * per + step
            at = slice(step * 128, (step + 1) * 128)
            spots = [cols[b, n] for n in range(listed)]
            pens = [
                bias[spots[n]] + jnp.where(same[b, n] == 1, 0.0, LOW) for n in range(listed)
            ]
            first = jnp.where(diagonal, 0.0, jnp.broadcast_to(pens[0], (128, 128)))
            for h in range(heads):
                query = qkv[part, h, :, at].astype(F32).T.astype(BF16)
                key_t = jnp.concatenate(
                    [keys[h, :, pl.ds(pl.multiple_of(s * 128, 128), 128)] for s in spots], axis=1
                )
                val = jnp.concatenate(
                    [vals[h, pl.ds(pl.multiple_of(s * 128, 128), 128), :] for s in spots], axis=0
                )
                scores = jnp.dot(query, key_t, preferred_element_type=F32) * (SCALE * LOG2E)
                scores = jnp.concatenate(
                    [scores[:, :128] + first]
                    + [scores[:, n * 128 : (n + 1) * 128] + pens[n] for n in range(1, listed)],
                    axis=1,
                )
                largest = jnp.max(scores, axis=1, keepdims=True)
                expd = jnp.exp2(scores - largest)
                probs = expd * (1.0 / jnp.sum(expd, axis=1, keepdims=True))
                probs = probs.astype(BF16)
                probs_out[h, b] = probs
                att = jnp.dot(probs, val, preferred_element_type=F32)
                att_out[part][h, :, at] = att.T.astype(BF16)


def backward_kernel(parts, heads, order, cols, index, qkv, probs_in, *refs):
    rows, d_att, out = refs[:parts], refs[parts : 2 * parts], refs[2 * parts : 3 * parts]
    sent, kept, keys, keys_t, vals_t, acc, whole = refs[3 * parts :]
    width = qkv.shape[3]
    group = heads * HD
    for k in range(parts):
        span = slice(k * width, (k + 1) * width)
        for h in range(heads):
            keys[h, span, :] = qkv[k, heads + h].astype(F32).T.astype(BF16)
            keys_t[h, :, span] = qkv[k, heads + h]
            vals_t[h, :, span] = qkv[k, 2 * heads + h]
    acc[group:, :] = jnp.zeros_like(acc[group:, :])
    count, listed = cols.shape
    per = count // parts
    for part in range(parts):

        for step in range(per):
            b = part * per + step
            at = slice(step * 128, (step + 1) * 128)
            into = slice(b * 128, (b + 1) * 128)
            spots = [
                pl.ds(pl.multiple_of(cols[b, n] * 128, 128), 128) for n in range(listed)
            ]
            for h in range(heads):
                d_t = d_att[part][h, :, at]
                query_t = qkv[part, h, :, at]
                val_t = jnp.concatenate([vals_t[h, :, s] for s in spots], axis=1)
                key = jnp.concatenate([keys[h, s, :] for s in spots], axis=0)
                d_probs = jnp.dot(
                    d_t.astype(F32).T.astype(BF16), val_t, preferred_element_type=F32
                )
                probs_low = probs_in[h, b]
                probs = probs_low.astype(F32)
                weighted = probs * d_probs
                delta = jnp.sum(weighted, axis=1, keepdims=True)
                d_scores = (probs * (d_probs - delta)).astype(BF16)
                d_query = jnp.dot(d_scores, key, preferred_element_type=F32)
                acc[h * HD : (h + 1) * HD, into] = d_query.T * SCALE
                d_key = jnp.dot(query_t, d_scores, preferred_element_type=F32)
                d_val = jnp.dot(d_t, probs_low, preferred_element_type=F32)
                for n in range(listed):
                    block = slice(n * 128, (n + 1) * 128)
                    acc[(heads + h) * HD : (heads + h + 1) * HD, spots[n]] += d_key[:, block]
                    acc[(2 * heads + h) * HD : (2 * heads + h + 1) * HD, spots[n]] += d_val[:, block]

    acc[group : 2 * group, :] = acc[group : 2 * group, :] * SCALE
    left = acc[...].astype(BF16)
    for k in range(parts):
        out[k][...] = left[:, k * width : (k + 1) * width]
    total = rows[0].shape[1]
    for start in range(0, total, 256):
        span = slice(start, min(start + 256, total))
        right = jnp.concatenate([row[:, span] for row in rows], axis=0)
        store_rows(whole, start, jnp.dot(left, right, preferred_element_type=F32).T)
    emit_halves(index, whole, order, sent, kept)


def traded(pieces):
    count = len(pieces)
    return [pieces[0]] + [shifted(pieces[count - j], count - j) for j in range(1, count)]


def body(tokens, weights, cotangent, col_list, cut_lengths, keep_mask):
    parts, replicas = lax.axis_size("seq"), lax.axis_size("dp")
    z = lax.axis_index("seq")
    place = z.astype(jnp.int32).reshape(1)
    index = lax.axis_index("dp").astype(jnp.int32).reshape(1)
    inputs, upstream = tokens[0], cotangent[0]
    width, model = inputs.shape
    shard, _, wide = weights.shape
    group = wide // parts
    heads = group // HD
    orders = bit_orders(replicas)
    length = parts * width

    columns = col_list[0]
    count, listed = columns.shape
    turn = z * (count // parts)
    columns = jnp.roll((columns - turn) % count, -turn, axis=0)
    ends = jnp.cumsum(cut_lengths[0])
    spots = (jnp.arange(count, dtype=jnp.int32) + turn) % count
    owner = jnp.sum((ends[None, :] <= spots[:, None]).astype(jnp.int32), axis=1)
    same = (owner[columns] == owner[:, None]).astype(jnp.int32)
    bias = jnp.where(jnp.roll(keep_mask[0].reshape(count, 1, -1), -turn, axis=0) == 1, 0.0, LOW)

    low, high = call(
        functools.partial(shard_kernel, parts), (shape_of(shard, 2 * wide),) * 2, [],
        "ordered_shard", [place], [weights],
    )

    far = far_indices(orders)
    single = [r for r in far if bin(r).count("1") == 1]
    several = [r for r in far if bin(r).count("1") > 1]
    pieces = hop([inputs])
    lows = {r: [exchanged(low, r)] for r in [1] + single}
    lows[0] = [low]
    parted = [parted_for(lows, r, orders) for r in several]
    mark = call(mark_kernel, shape_of(8, 128), [], "mark", [], [pieces[1][:8, :128]], flops=1 << 34)
    pieces, lows, parted, mark = together(pieces, lows, parted, mark)

    while len(pieces) < parts - 1:
        pieces = hop(pieces)
    passed_on(lows, several, parted, orders)
    lows, high = together(lows, high)
    highs = {r: [exchanged(high, r)] for r in single}
    for r in far[1:]:
        lows[r | 1] = [exchanged(piece, 1) for piece in lows[r]]
    mark = call(mark_kernel, shape_of(8, 128), [], "mark", [], [pieces[-1][:8, :128]], flops=1 << 34)
    pieces, lows, mark = together(pieces, lows, mark)

    pieces = hop(pieces)
    low = in_order(lows, index)
    highs[0] = [high]
    highs, low = together(highs, low)
    passed_on(highs, several, [parted_for(highs, r, orders) for r in several], orders)
    for r in single:
        highs[r | 1] = [exchanged(highs[r][0], 1)]
    early = call(
        functools.partial(early_kernel, parts), shape_of(parts - 1, 3 * heads, HD, width),
        [], "early", [], [low] + pieces[:-1],
    )
    d_att = call(
        functools.partial(project_kernel, parts, group),
        (shape_of(group, width),) * parts, [], "project", [], [upstream, low],
    )
    pieces, d_att, early, highs = together(pieces, d_att, early, highs)

    d_att = [d.reshape(heads, HD, width) for d in traded(d_att)]
    results = call(
        functools.partial(forward_kernel, parts, heads),
        (shape_of(parts, 3 * heads, HD, width),)
        + (shape_of(heads, HD, width),) * parts
        + (shape_of(heads, count, 128, listed * 128),),
        [pltpu.VMEM((heads, HD, length), BF16), pltpu.VMEM((heads, length, HD), BF16)],
        "attend", [columns, same], [bias, low, pieces[-1], early],
        flops=1 << 34,
    )
    d_att, results, highs = together(d_att, results, highs)
    qkv, att, probs = results[0], results[1:-1], results[-1]

    att = traded([a.reshape(group, width) for a in att])
    halved = (replicas // 2, shard, 3 * group)
    back = call(
        functools.partial(backward_kernel, parts, heads, orders[0]),
        (shape_of(3 * group, width),) * parts + (shape_of(*halved), shape_of(*halved, dtype=F32)),
        [
            pltpu.VMEM((heads, length, HD), BF16),
            pltpu.VMEM((heads, HD, length), BF16),
            pltpu.VMEM((heads, HD, length), BF16),
            pltpu.VMEM((3 * group, length), F32),
            pltpu.VMEM((replicas, shard, 3 * group), F32),
        ],
        "attend_back", [columns, index], [qkv, probs] + pieces + list(d_att), flops=1 << 34, limit=24,
    )
    highs[1] = [exchanged(high, 1)]
    att, back, highs = together(att, back, highs)
    for r in several:
        highs[r | 1] = [exchanged(piece, 1) for piece in highs[r]]

    d_qkv, sent, inner_sum = back[:parts], back[parts], back[parts + 1]
    d_here = [d_qkv[0]] + [None] * (parts - 1)
    def fetch(which):
        for j in which:
            d_here[j] = shifted(d_qkv[parts - j], parts - j)

    fetch([1, parts - 1])
    inner_more = exchanged(sent, 1)
    sent, outer_sum = gradient_halves(
        functools.partial(outer_gradient_kernel, parts, orders[0]), "outer_gradient", wide,
        [index], [upstream] + list(att), replicas,
    )
    outer_more = exchanged(sent, 1)
    cut = 3 * group
    away = block_order(orders[0])[:-1]
    kept, *given = call(
        functools.partial(combine_kernel, cut),
        (shape_of(shard, cut + wide, dtype=F32),) + (shape_of(shard, cut + wide),) * len(away),
        [], "combine", [], [inner_sum, inner_more, outer_sum, outer_more], flops=1 << 33,
    )
    arrived = [exchanged(piece, r) for piece, r in zip(given, away)]
    d_qkv, d_here[1], d_here[-1] = together(d_qkv, d_here[1], d_here[-1])
    fetch(range(2, parts - 1))
    inner_own, *pieces = call(
        functools.partial(finish_kernel, cut, group),
        (shape_of(shard, cut),) + (shape_of(shard // 2, 2 * group),) * parts,
        [], "finish", [], [kept] + arrived,
    )
    pieces, d_here = together(pieces, d_here)

    own = call(
        own_kernel, shape_of(shard // 2, 2 * (cut + group)), [], "own", [], [inner_own] + traded(pieces)
    )
    own, att = together(own, att)
    found = [own] + [shifted(own, parts - j) for j in range(1, parts)]
    result = call(
        functools.partial(result_kernel, parts, group),
        shape_of(width, model), [pltpu.VMEM((wide, width), F32)], "result", [],
        [low] + list(att), flops=1 << 32,
    )
    high = in_order(highs, index)
    grad_in = call(
        functools.partial(grad_in_kernel, parts, group),
        shape_of(width, model), [pltpu.VMEM((3 * wide, width), F32)],
        "grad_in", [], [low, high] + list(d_here), flops=1 << 33, limit=20,
    )
    grad_all = call(
        functools.partial(final_kernel, parts, replicas),
        shape_of(shard, 4, wide, dtype=F32), [], "final_rows", [place], found,
    )
    return (result[None], grad_in[None], grad_all)


def solution(mesh):
    placed = (
        P("dp", "seq", None),
        P("dp", None, None),
        P("dp", "seq", None),
        P("dp", None, None),
        P("dp", None),
        P("dp", None),
    )
    return jax.shard_map(
        body,
        mesh=mesh,
        in_specs=placed,
        out_specs=(P("dp", "seq", None), P("dp", "seq", None), P("dp", None, None)),
        check_vma=False,
    )
```

```python
import functools
import math

import jax
import jax.numpy as jnp
from jax import lax
from jax.experimental import pallas as pl
from jax.experimental.pallas import tpu as pltpu
from jax.sharding import PartitionSpec as P

HD = 88
SCALE = 1.0 / math.sqrt(HD)
LOG2E = math.log2(math.e)
LOW = -1e30
F32 = jnp.float32
BF16 = jnp.bfloat16


def shifted(array, step):
    count = lax.axis_size("seq")
    return lax.ppermute(array, "seq", [(i, (i + step) % count) for i in range(count)])


def exchanged(array, bit):
    count = lax.axis_size("dp")
    return lax.ppermute(array, "dp", [(i, i ^ bit) for i in range(count)])


def bit_orders(count):
    far = [1 << i for i in range(1, count.bit_length() - 1)]
    half = len(far) // 2
    return far, far[half:] + far[:half]


def block_order(bits):
    if not bits:
        return [0]
    rest = block_order(bits[1:])
    return [r | bits[0] for r in rest] + rest


VMEM = pl.BlockSpec(memory_space=pltpu.VMEM)
SMEM = pl.BlockSpec(memory_space=pltpu.SMEM)


def call(kernel, out_shape, scratch, name, scalars, arrays, flops=1, limit=16):
    single = not isinstance(out_shape, tuple)
    return pl.pallas_call(
        kernel,
        out_shape=out_shape,
        in_specs=[SMEM] * len(scalars) + [VMEM] * len(arrays),
        out_specs=VMEM if single else (VMEM,) * len(out_shape),
        scratch_shapes=scratch,
        compiler_params=pltpu.CompilerParams(vmem_limit_bytes=limit << 20),
        cost_estimate=pl.CostEstimate(flops=flops, bytes_accessed=1, transcendentals=0),
        name=name,
    )(*scalars, *arrays)


def together(*trees):
    return lax.optimization_barrier(trees)


def shape_of(*dims, dtype=BF16):
    return jax.ShapeDtypeStruct(dims, dtype)


def far_indices(orders):
    return sorted(range(0, 2 << len(orders[0]), 2), key=lambda r: (bin(r).count("1"), r))


def parting_kernel(spans, *refs):
    count = len(spans)
    for span, piece, out in zip(spans, refs[:count], refs[count:]):
        out[...] = piece[:, span]


def parted_for(held, r, orders):
    half = held[0][0].shape[1] // 2
    parts = []
    for n, order in enumerate(orders):
        source = held.get(r ^ max((b for b in order if b & r), key=order.index))
        if source is None:
            return None
        whole = len(source) == 1
        parts.append((source[0], slice(n * half, (n + 1) * half)) if whole else (source[n], slice(None)))
    return call(
        functools.partial(parting_kernel, [span for _, span in parts]),
        (shape_of(parts[0][0].shape[0], half),) * 2, [], "parting", [],
        [piece for piece, _ in parts],
    )


def passed_on(held, several, parted, orders):
    for r, halves in zip(several, parted):
        halves = halves or parted_for(held, r, orders)
        last = [max((b for b in order if b & r), key=order.index) for order in orders]
        held[r] = [exchanged(halves[n], last[n]) for n in range(2)]


def in_order_kernel(sizes, index, *refs):
    pieces, out, at = refs[:-1], refs[-1], 0
    half = out.shape[2] // 2
    for r, size in sizes:
        if size == 1:
            out[index[0] ^ r] = pieces[at][...]
        else:
            out[index[0] ^ r, :, :half] = pieces[at][...]
            out[index[0] ^ r, :, half:] = pieces[at + 1][...]
        at += size


def in_order(held, index, flops=1):
    count, (rows, columns) = len(held), held[0][0].shape
    out = call(
        functools.partial(in_order_kernel, [(r, len(held[r])) for r in held]),
        shape_of(count, rows, columns), [], "in_order", [index],
        [piece for r in held for piece in held[r]], flops=flops,
    )
    return out.reshape(count * rows, columns)


def mark_kernel(piece, out):
    out[...] = piece[...]


def shard_kernel(parts, place, weights, low, high):
    group = weights.shape[2] // parts
    for z in range(parts):

        @pl.when(place[0] == z)
        def _():
            cols = [weights[:, c, :] for c in range(4)]

            def block(c, j):
                start = (z + j) % parts * group
                return cols[c][:, start : start + group]

            chosen = [block(c, 0) for c in range(3)] + [block(3, j) for j in range(parts)]
            chosen += [block(c, j) for j in range(1, parts) for c in range(3)]
            low[...] = jnp.concatenate(chosen[: 2 * parts], axis=1)
            high[...] = jnp.concatenate(chosen[2 * parts :], axis=1)


def project_kernel(parts, group, rows, low, *out):
    outer = low[:, 3 * group : (3 + parts) * group]
    total = jnp.dot(rows[...], outer, preferred_element_type=F32).T
    for j in range(parts):
        out[j][...] = total[j * group : (j + 1) * group].astype(BF16)


def result_kernel(parts, group, low, *refs):
    att, (out, scratch) = refs[:parts], refs[parts:]
    for j in range(parts):
        scratch[j * group : (j + 1) * group, :] = att[j][...].astype(F32)
    left = scratch[...].T.astype(BF16)
    outer = low[:, 3 * group : (3 + parts) * group]
    out[...] = lax.dot_general(
        left, outer, (((1,), (1,)), ((), ())), preferred_element_type=F32
    ).astype(BF16)


def grad_in_kernel(parts, group, low, high, *refs):
    d_here, (out, scratch) = refs[:parts], refs[parts:]
    for j in range(parts):
        scratch[j * 3 * group : (j + 1) * 3 * group, :] = d_here[j][...].astype(F32)
    left = scratch[...].T.astype(BF16)
    first, rest = 3 * group, left.shape[1] - high.shape[1]
    contract = (((1,), (1,)), ((), ()))
    total = lax.dot_general(
        left[:, rest:], high[...], contract, preferred_element_type=F32
    )
    total += lax.dot_general(
        left[:, :first], low[:, :first], contract, preferred_element_type=F32
    )
    if rest > first:
        total += lax.dot_general(
            left[:, first:rest], low[:, (3 + parts) * group :], contract,
            preferred_element_type=F32,
        )
    out[...] = total.astype(BF16)


def store_rows(whole, start, value):
    rows, end = whole.shape[1], start + value.shape[0]
    at = start
    while at < end:
        block, first = divmod(at, rows)
        size = min(rows - first, end - at)
        whole[block, first : first + size, :] = value[at - start : at - start + size]
        at += size


def emit_halves(index, whole, order, sent, kept):
    for i, r in enumerate(block_order(order)):
        mine = index[0] ^ r
        kept[i] = whole[mine]
        sent[i] = whole[mine ^ 1].astype(BF16)


def outer_gradient_kernel(parts, order, index, rows, *refs):
    att, (sent, kept, whole) = refs[:parts], refs[parts:]
    left = jnp.concatenate([a[...] for a in att], axis=0)
    for start in range(0, rows.shape[1], 256):
        span = slice(start, min(start + 256, rows.shape[1]))
        store_rows(whole, start, jnp.dot(left, rows[:, span], preferred_element_type=F32).T)
    emit_halves(index, whole, order, sent, kept)


def gradient_halves(kernel, name, columns, scalars, arrays, replicas):
    width = arrays[0].shape[-1]
    shape = (replicas // 2, width // replicas, columns)
    return call(
        kernel, (shape_of(*shape), shape_of(*shape, dtype=F32)),
        [pltpu.VMEM((replicas, width // replicas, columns), F32)], name, scalars, arrays, flops=1 << 34,
    )


def combine_kernel(cut, inner, inner_more, outer, outer_more, kept, *out):
    count = inner.shape[0]
    for i in range(count):
        left = inner[i] + inner_more[i].astype(F32)
        right = outer[i] + outer_more[i].astype(F32)
        if i < count - 1:
            out[i][:, :cut] = left.astype(BF16)
            out[i][:, cut:] = right.astype(BF16)
        else:
            kept[:, :cut] = left
            kept[:, cut:] = right


def finish_kernel(cut, group, kept, *refs):
    parts = (kept.shape[1] - cut) // group
    arrived, (inner, *outer) = refs[: -parts - 1], refs[-parts - 1 :]
    total = kept[...]
    for more in arrived:
        total += more[...].astype(F32)
    half = total.shape[0] // 2
    inner[...] = total[:, :cut].astype(BF16)
    for j in range(parts):
        span = slice(cut + j * group, cut + (j + 1) * group)
        outer[j][...] = jnp.concatenate([total[:half, span], total[half:, span]], axis=1).astype(BF16)


def own_kernel(inner, *refs):
    pieces, out = refs[:-1], refs[-1]
    half, group = pieces[0].shape[0], pieces[0].shape[1] // 2
    total = pieces[0][...].astype(F32)
    for piece in pieces[1:]:
        total += piece[...].astype(F32)
    first = inner[...].astype(F32)
    out[...] = jnp.concatenate(
        [first[:half], total[:, :group], first[half:], total[:, group:]], axis=1
    ).astype(BF16)


def final_kernel(parts, replicas, place, *refs):
    found, out = refs[:-1], refs[-1]
    group = out.shape[2] // parts
    for z in range(parts):

        @pl.when(place[0] == z)
        def _():
            turn = [(hg - z) % parts for hg in range(parts)]
            half, wide = found[0].shape[0], found[0].shape[1] // 2
            for c in range(4):
                for n in range(2):
                    span = slice(n * wide + c * group, n * wide + (c + 1) * group)
                    out[n * half : (n + 1) * half, c, :] = jnp.concatenate(
                        [found[j][:, span].astype(F32) for j in turn], axis=1
                    ) * (1.0 / replicas)


def hop(pieces):
    return pieces + [shifted(pieces[-1], -1)]


def store_projection(qkv, k, rows, own):
    total = jnp.dot(rows[...], own, preferred_element_type=F32).T
    for i in range(qkv.shape[1]):
        qkv[k, i] = total[i * HD : (i + 1) * HD].astype(BF16)


def early_kernel(parts, low, *refs):
    pieces, qkv = refs[: parts - 1], refs[-1]
    own = low[:, : qkv.shape[1] * HD]
    for k in range(parts - 1):
        store_projection(qkv, k, pieces[k], own)


def forward_kernel(parts, heads, cols, same, bias, low, piece, early, *refs):
    qkv, att_out = refs[0], refs[1 : parts + 1]
    probs_out, keys, vals = refs[parts + 1 :]
    group, width = heads * HD, qkv.shape[3]
    for k in range(parts - 1):
        qkv[k] = early[k]
    store_projection(qkv, parts - 1, piece, low[:, : 3 * group])
    for k in range(parts):
        span = slice(k * width, (k + 1) * width)
        for h in range(heads):
            keys[h, :, span] = qkv[k, heads + h]
            vals[h, span, :] = qkv[k, 2 * heads + h].astype(F32).T.astype(BF16)
    count, listed = cols.shape
    per = count // parts
    line = lax.broadcasted_iota(jnp.int32, (128, 128), 0)
    lanes = lax.broadcasted_iota(jnp.int32, (128, 128), 1)
    diagonal = line == lanes
    for part in range(parts):

        for step in range(per):
            b = part * per + step
            at = slice(step * 128, (step + 1) * 128)
            spots = [cols[b, n] for n in range(listed)]
            pens = [
                bias[spots[n]] + jnp.where(same[b, n] == 1, 0.0, LOW) for n in range(listed)
            ]
            first = jnp.where(diagonal, 0.0, jnp.broadcast_to(pens[0], (128, 128)))
            for h in range(heads):
                query = qkv[part, h, :, at].astype(F32).T.astype(BF16)
                key_t = jnp.concatenate(
                    [keys[h, :, pl.ds(pl.multiple_of(s * 128, 128), 128)] for s in spots], axis=1
                )
                val = jnp.concatenate(
                    [vals[h, pl.ds(pl.multiple_of(s * 128, 128), 128), :] for s in spots], axis=0
                )
                scores = jnp.dot(query, key_t, preferred_element_type=F32) * (SCALE * LOG2E)
                scores = jnp.concatenate(
                    [scores[:, :128] + first]
                    + [scores[:, n * 128 : (n + 1) * 128] + pens[n] for n in range(1, listed)],
                    axis=1,
                )
                largest = jnp.max(scores, axis=1, keepdims=True)
                expd = jnp.exp2(scores - largest)
                probs = expd * (1.0 / jnp.sum(expd, axis=1, keepdims=True))
                probs = probs.astype(BF16)
                probs_out[h, b] = probs
                att = jnp.dot(probs, val, preferred_element_type=F32)
                att_out[part][h, :, at] = att.T.astype(BF16)


def backward_kernel(parts, heads, order, cols, index, qkv, probs_in, *refs):
    rows, d_att, out = refs[:parts], refs[parts : 2 * parts], refs[2 * parts : 3 * parts]
    sent, kept, keys, keys_t, vals_t, acc, whole = refs[3 * parts :]
    width = qkv.shape[3]
    group = heads * HD
    for k in range(parts):
        span = slice(k * width, (k + 1) * width)
        for h in range(heads):
            keys[h, span, :] = qkv[k, heads + h].astype(F32).T.astype(BF16)
            keys_t[h, :, span] = qkv[k, heads + h]
            vals_t[h, :, span] = qkv[k, 2 * heads + h]
    acc[group:, :] = jnp.zeros_like(acc[group:, :])
    count, listed = cols.shape
    per = count // parts
    for part in range(parts):

        for step in range(per):
            b = part * per + step
            at = slice(step * 128, (step + 1) * 128)
            into = slice(b * 128, (b + 1) * 128)
            spots = [
                pl.ds(pl.multiple_of(cols[b, n] * 128, 128), 128) for n in range(listed)
            ]
            for h in range(heads):
                d_t = d_att[part][h, :, at]
                query_t = qkv[part, h, :, at]
                val_t = jnp.concatenate([vals_t[h, :, s] for s in spots], axis=1)
                key = jnp.concatenate([keys[h, s, :] for s in spots], axis=0)
                d_probs = jnp.dot(
                    d_t.astype(F32).T.astype(BF16), val_t, preferred_element_type=F32
                )
                probs_low = probs_in[h, b]
                probs = probs_low.astype(F32)
                weighted = probs * d_probs
                delta = jnp.sum(weighted, axis=1, keepdims=True)
                d_scores = (probs * (d_probs - delta)).astype(BF16)
                d_query = jnp.dot(d_scores, key, preferred_element_type=F32)
                acc[h * HD : (h + 1) * HD, into] = d_query.T * SCALE
                d_key = jnp.dot(query_t, d_scores, preferred_element_type=F32)
                d_val = jnp.dot(d_t, probs_low, preferred_element_type=F32)
                for n in range(listed):
                    block = slice(n * 128, (n + 1) * 128)
                    acc[(heads + h) * HD : (heads + h + 1) * HD, spots[n]] += d_key[:, block]
                    acc[(2 * heads + h) * HD : (2 * heads + h + 1) * HD, spots[n]] += d_val[:, block]

    acc[group : 2 * group, :] = acc[group : 2 * group, :] * SCALE
    left = acc[...].astype(BF16)
    for k in range(parts):
        out[k][...] = left[:, k * width : (k + 1) * width]
    total = rows[0].shape[1]
    for start in range(0, total, 256):
        span = slice(start, min(start + 256, total))
        right = jnp.concatenate([row[:, span] for row in rows], axis=0)
        store_rows(whole, start, jnp.dot(left, right, preferred_element_type=F32).T)
    emit_halves(index, whole, order, sent, kept)


def traded(pieces):
    count = len(pieces)
    return [pieces[0]] + [shifted(pieces[count - j], count - j) for j in range(1, count)]


def body(tokens, weights, cotangent, col_list, cut_lengths, keep_mask):
    parts, replicas = lax.axis_size("seq"), lax.axis_size("dp")
    z = lax.axis_index("seq")
    place = z.astype(jnp.int32).reshape(1)
    index = lax.axis_index("dp").astype(jnp.int32).reshape(1)
    inputs, upstream = tokens[0], cotangent[0]
    width, model = inputs.shape
    shard, _, wide = weights.shape
    group = wide // parts
    heads = group // HD
    orders = bit_orders(replicas)
    length = parts * width

    columns = col_list[0]
    count, listed = columns.shape
    turn = z * (count // parts)
    columns = jnp.roll((columns - turn) % count, -turn, axis=0)
    ends = jnp.cumsum(cut_lengths[0])
    spots = (jnp.arange(count, dtype=jnp.int32) + turn) % count
    owner = jnp.sum((ends[None, :] <= spots[:, None]).astype(jnp.int32), axis=1)
    same = (owner[columns] == owner[:, None]).astype(jnp.int32)
    bias = jnp.where(jnp.roll(keep_mask[0].reshape(count, 1, -1), -turn, axis=0) == 1, 0.0, LOW)

    low, high = call(
        functools.partial(shard_kernel, parts), (shape_of(shard, 2 * wide),) * 2, [],
        "ordered_shard", [place], [weights],
    )

    far = far_indices(orders)
    single = [r for r in far if bin(r).count("1") == 1]
    several = [r for r in far if bin(r).count("1") > 1]
    pieces = hop([inputs])
    lows = {r: [exchanged(low, r)] for r in [1] + single}
    lows[0] = [low]
    parted = [parted_for(lows, r, orders) for r in several]
    mark = call(mark_kernel, shape_of(8, 128), [], "mark", [], [pieces[1][:8, :128]], flops=1 << 34)
    pieces, lows, parted, mark = together(pieces, lows, parted, mark)

    while len(pieces) < parts - 1:
        pieces = hop(pieces)
    passed_on(lows, several, parted, orders)
    lows, high = together(lows, high)
    highs = {r: [exchanged(high, r)] for r in single}
    for r in far[1:]:
        lows[r | 1] = [exchanged(piece, 1) for piece in lows[r]]
    mark = call(mark_kernel, shape_of(8, 128), [], "mark", [], [pieces[-1][:8, :128]], flops=1 << 34)
    pieces, lows, mark = together(pieces, lows, mark)

    pieces = hop(pieces)
    low = in_order(lows, index)
    highs[0] = [high]
    highs, low = together(highs, low)
    for r in [0] + single:
        highs[r | 1] = [exchanged(highs[r][0], 1)]
    early = call(
        functools.partial(early_kernel, parts), shape_of(parts - 1, 3 * heads, HD, width),
        [], "early", [], [low] + pieces[:-1],
    )
    d_att = call(
        functools.partial(project_kernel, parts, group),
        (shape_of(group, width),) * parts, [], "project", [], [upstream, low],
    )
    pieces, d_att, early, highs = together(pieces, d_att, early, highs)

    d_att = [d.reshape(heads, HD, width) for d in traded(d_att)]
    results = call(
        functools.partial(forward_kernel, parts, heads),
        (shape_of(parts, 3 * heads, HD, width),)
        + (shape_of(heads, HD, width),) * parts
        + (shape_of(heads, count, 128, listed * 128),),
        [pltpu.VMEM((heads, HD, length), BF16), pltpu.VMEM((heads, length, HD), BF16)],
        "attend", [columns, same], [bias, low, pieces[-1], early],
        flops=1 << 34,
    )
    d_att, results, highs = together(d_att, results, highs)
    qkv, att, probs = results[0], results[1:-1], results[-1]

    att = traded([a.reshape(group, width) for a in att])
    halved = (replicas // 2, shard, 3 * group)
    back = call(
        functools.partial(backward_kernel, parts, heads, orders[0]),
        (shape_of(3 * group, width),) * parts + (shape_of(*halved), shape_of(*halved, dtype=F32)),
        [
            pltpu.VMEM((heads, length, HD), BF16),
            pltpu.VMEM((heads, HD, length), BF16),
            pltpu.VMEM((heads, HD, length), BF16),
            pltpu.VMEM((3 * group, length), F32),
            pltpu.VMEM((replicas, shard, 3 * group), F32),
        ],
        "attend_back", [columns, index], [qkv, probs] + pieces + list(d_att), flops=1 << 34, limit=24,
    )
    passed_on(highs, several, [parted_for(highs, r, orders) for r in several], orders)
    att, back, highs = together(att, back, highs)
    for r in several:
        highs[r | 1] = [exchanged(piece, 1) for piece in highs[r]]

    d_qkv, sent, inner_sum = back[:parts], back[parts], back[parts + 1]
    d_here = [d_qkv[0]] + [None] * (parts - 1)
    def fetch(which):
        for j in which:
            d_here[j] = shifted(d_qkv[parts - j], parts - j)

    fetch([1, parts - 1])
    inner_more = exchanged(sent, 1)
    sent, outer_sum = gradient_halves(
        functools.partial(outer_gradient_kernel, parts, orders[0]), "outer_gradient", wide,
        [index], [upstream] + list(att), replicas,
    )
    outer_more = exchanged(sent, 1)
    cut = 3 * group
    away = block_order(orders[0])[:-1]
    kept, *given = call(
        functools.partial(combine_kernel, cut),
        (shape_of(shard, cut + wide, dtype=F32),) + (shape_of(shard, cut + wide),) * len(away),
        [], "combine", [], [inner_sum, inner_more, outer_sum, outer_more], flops=1 << 33,
    )
    arrived = [exchanged(piece, r) for piece, r in zip(given, away)]
    d_qkv, d_here[1], d_here[-1] = together(d_qkv, d_here[1], d_here[-1])
    fetch(range(2, parts - 1))
    inner_own, *pieces = call(
        functools.partial(finish_kernel, cut, group),
        (shape_of(shard, cut),) + (shape_of(shard // 2, 2 * group),) * parts,
        [], "finish", [], [kept] + arrived,
    )
    pieces, d_here = together(pieces, d_here)

    own = call(
        own_kernel, shape_of(shard // 2, 2 * (cut + group)), [], "own", [], [inner_own] + traded(pieces)
    )
    own, att = together(own, att)
    found = [own] + [shifted(own, parts - j) for j in range(1, parts)]
    result = call(
        functools.partial(result_kernel, parts, group),
        shape_of(width, model), [pltpu.VMEM((wide, width), F32)], "result", [],
        [low] + list(att), flops=1 << 32,
    )
    high = in_order(highs, index)
    grad_in = call(
        functools.partial(grad_in_kernel, parts, group),
        shape_of(width, model), [pltpu.VMEM((3 * wide, width), F32)],
        "grad_in", [], [low, high] + list(d_here), flops=1 << 33, limit=20,
    )
    grad_all = call(
        functools.partial(final_kernel, parts, replicas),
        shape_of(shard, 4, wide, dtype=F32), [], "final_rows", [place], found,
    )
    return (result[None], grad_in[None], grad_all)


def solution(mesh):
    placed = (
        P("dp", "seq", None),
        P("dp", None, None),
        P("dp", "seq", None),
        P("dp", None, None),
        P("dp", None),
        P("dp", None),
    )
    return jax.shard_map(
        body,
        mesh=mesh,
        in_specs=placed,
        out_specs=(P("dp", "seq", None), P("dp", "seq", None), P("dp", None, None)),
        check_vma=False,
    )
```
